256 devices in a mesh: leaf: 64 (over z, x, core), blk: 4 (over y).
Axes of the slice: x: 4, y: 4, z: 8, core: 2. Of those that a mesh axis runs over, the one named last changes fastest.
Arguments:
- points: bfloat16 [64, 1024, 512], P(None, 'leaf', 'blk')
- charges: bfloat16 [16, 1024, 512], P(None, 'leaf', 'blk'), may hold values from -6 to 6
- leaf_interp: bfloat16 [1024, 256, 512], P('leaf'), may hold values from -0.25 to 0.25
- root_interp: bfloat16 [1024, 256, 256], P('leaf'), may hold values from -0.09375 to 0.09375
- skeleton_index: int32 [1024, 256], P('leaf'), may hold values from 0 to 511, as said below
- root_index: int32 [64, 256], P('leaf'), may hold values from 0 to 4095, as said below
- near_list: int32 [1024, 10], P('leaf'), may hold values from 0 to 1023, as said below
- far_list: int32 [1024, 32], P('leaf'), may hold values from 0 to 1023, as said below
- far_count: int32 [1024], P('leaf'), may hold values from 1 to 32, as said below
Outputs:
- potentials: float32 [16, 1024, 512], P(None, 'leaf', 'blk')
The draws below stay inside these ranges and needn't reach their ends.
Inputs may be any that keep to these rules, and one draw needn't show every extreme that they name: `skeleton_index`: each row names 256 different points of its leaf. `root_index`: row o names 256 different skeleton points of owner o, numbered leaf by leaf with 256 to a leaf. `near_list`: row l names 10 different leaves, l among them, all in the window of 17 consecutive leaves that begins at max(0, min(l - 8, 1007)); both ends of that window are named. `far_list`: leaf l belongs to owner o = l // 16; its first far_count[l] entries are different leaves of the existing owners among o - 2, o - 1, o + 1, o + 2, and its later entries repeat l and are not used; over the used entries of all leaves of one owner, each of those owners has exactly 8 different leaves named. `far_count`: at most the number of leaves that the owner's far lists can name (32 for owners at distance 2 or more from both ends); the first leaf of every owner uses all of them; the mean load differs strongly from owner to owner.
All inputs are finite; a program needn't handle non-finite values.
Results may differ from the reference program's by a relative error of at most 0.0036.
Values may be sent and summed in bfloat16 or wider, within the bound.
A program may use at most 128 MiB of HBM per device.

```python
import jax
import jax.numpy as jnp
from jax import lax

DIM = 64
RHS = 16
LEAF_PTS = 512
SKEL = 256
LEAF_DEV = 16
HALO = 8
NEAR = 10
CAP = 8
FAR = 32
LEAVES = 1024
N_LEAF = 64


def distinct_prefix(key, row_count, pool_size, keep_count):
    scores = jax.random.randint(key, (row_count, pool_size), 0, (1 << 30) // pool_size)
    scores = scores * pool_size + jnp.arange(pool_size, dtype=jnp.int32)[None, :]
    return jnp.argsort(scores, axis=1)[:, :keep_count].astype(jnp.int32)


def far_tables(key):
    pool_key, order_key, level_key, count_key = jax.random.split(key, 4)
    owner_steps = jnp.array([-2, -1, 1, 2], jnp.int32)
    pool_scores = jax.random.randint(pool_key, (N_LEAF, 4, LEAF_DEV), 0, 1 << 20) * LEAF_DEV + jnp.arange(LEAF_DEV, dtype=jnp.int32)
    pool_members = jnp.argsort(pool_scores, axis=2)[:, :, :CAP].astype(jnp.int32)
    target_owner = jnp.arange(N_LEAF, dtype=jnp.int32)[:, None] + owner_steps[None, :]
    exists = (target_owner >= 0) & (target_owner < N_LEAF)
    candidates = (target_owner[:, :, None] * LEAF_DEV + pool_members).reshape(N_LEAF, FAR)
    candidate_ok = jnp.repeat(exists, CAP, axis=1)
    leaf_owner = jnp.arange(LEAVES, dtype=jnp.int32) // LEAF_DEV
    leaf_candidates = candidates[leaf_owner]
    leaf_ok = candidate_ok[leaf_owner]
    order_scores = jax.random.randint(order_key, (LEAVES, FAR), 0, 1 << 20) * FAR + jnp.arange(FAR, dtype=jnp.int32)[None, :]
    order_scores = order_scores + jnp.where(leaf_ok, 0, (1 << 20) * FAR)
    order_index = jnp.argsort(order_scores, axis=1)
    sorted_ids = jnp.take_along_axis(leaf_candidates, order_index, axis=1)
    usable = jnp.sum(leaf_ok.astype(jnp.int32), axis=1)
    levels = 2 ** jax.random.randint(level_key, (N_LEAF,), 1, 6)
    counts = 1 + jax.random.randint(count_key, (LEAVES,), 0, levels[leaf_owner])
    counts = jnp.minimum(counts, usable)
    first_of_owner = jnp.arange(LEAVES, dtype=jnp.int32) % LEAF_DEV == 0
    counts = jnp.where(first_of_owner, usable, counts).astype(jnp.int32)
    slot_ids = jnp.arange(FAR, dtype=jnp.int32)[None, :]
    far_ids = jnp.where(slot_ids < counts[:, None], sorted_ids, jnp.arange(LEAVES, dtype=jnp.int32)[:, None]).astype(jnp.int32)
    return (far_ids, counts)


def draw_points(key, part):
    key = jax.random.fold_in(key, 11)
    scale_key, value_key = jax.random.split(key)
    scales = jnp.exp(jax.random.uniform(scale_key, (DIM, 1, 1), jnp.float32, jnp.log(0.02), jnp.log(0.6)))
    values = jax.random.normal(value_key, (DIM, LEAVES, LEAF_PTS), jnp.float32)
    return (values * scales).astype(jnp.bfloat16)


def draw_skeleton_index(key, part):
    key = jax.random.fold_in(key, 12)
    return distinct_prefix(key, LEAVES, LEAF_PTS, SKEL)


def draw_root_index(key, part):
    key = jax.random.fold_in(key, 13)
    return distinct_prefix(key, N_LEAF, LEAF_DEV * SKEL, SKEL)


def draw_near_list(key, part):
    key = jax.random.fold_in(key, 14)
    score_key, shuffle_key = jax.random.split(key)
    window = 2 * HALO + 1
    leaf_ids = jnp.arange(LEAVES, dtype=jnp.int32)
    window_start = jnp.clip(leaf_ids - HALO, 0, LEAVES - window)
    own_offset = leaf_ids - window_start
    offsets = jnp.arange(window, dtype=jnp.int32)[None, :]
    base_scores = jax.random.randint(score_key, (LEAVES, window), 0, 1 << 20) * window + offsets + 3
    scores = jnp.where(offsets == window - 1, 2, base_scores)
    scores = jnp.where(offsets == 0, 1, scores)
    scores = jnp.where(offsets == own_offset[:, None], 0, scores)
    chosen = jnp.argsort(scores, axis=1)[:, :NEAR].astype(jnp.int32)
    shuffle_scores = jax.random.randint(shuffle_key, (LEAVES, NEAR), 0, 1 << 20) * NEAR + jnp.arange(NEAR, dtype=jnp.int32)[None, :]
    shuffled = jnp.take_along_axis(chosen, jnp.argsort(shuffle_scores, axis=1), axis=1)
    return (window_start[:, None] + shuffled).astype(jnp.int32)


def draw_far_list(key, part):
    return far_tables(key)[0]


def draw_far_count(key, part):
    return far_tables(key)[1]


def level_of(stream_key, shape, shards, smallest, top_value):
    def one(position, blocks):
        heights = jax.random.uniform(jax.random.fold_in(jax.random.fold_in(stream_key, 6), position), (blocks,), jnp.float32, smallest / len(shards), top_value / len(shards))
        return jnp.repeat(jnp.exp(heights), shape[position] // blocks).reshape((-1,) + (1,) * (len(shape) - position - 1))

    gain = one(*shards[0])
    for cut in shards[1:]:
        gain = gain * one(*cut)
    return gain


def noise(rng, extent, spread, bound, cuts=(), kind=jnp.bfloat16):
    values = jax.random.normal(rng, extent, jnp.float32) * spread
    if len(cuts) > 0:
        values = level_of(rng, extent, cuts, -0.22, 0.18) * values
    return jnp.clip(values, min=-bound, max=bound).astype(kind)


def setup_inputs(seed: int = 0) -> dict:
    key_of = jax.random.split(jax.random.key(seed), 10)
    points = draw_points(jax.random.fold_in(key_of[9], 71), 0)
    charges = noise(key_of[1], (RHS, LEAVES, LEAF_PTS), 1.0, 6.0, ((1, 64), (2, 4)))
    leaf_interp = noise(key_of[2], (LEAVES, SKEL, LEAF_PTS), LEAF_PTS ** -0.5, 0.25, ((0, 64),))
    root_interp = noise(key_of[3], (LEAVES, SKEL, SKEL), (LEAF_DEV * SKEL) ** -0.5, 0.09375, ((0, 64),))
    skeleton_index = draw_skeleton_index(jax.random.fold_in(key_of[9], 71), 0)
    root_index = draw_root_index(jax.random.fold_in(key_of[9], 71), 0)
    near_list = draw_near_list(jax.random.fold_in(key_of[9], 71), 0)
    far_list = draw_far_list(jax.random.fold_in(key_of[9], 71), 0)
    far_count = draw_far_count(jax.random.fold_in(key_of[9], 71), 0)
    return {"points": points, "charges": charges, "leaf_interp": leaf_interp, "root_interp": root_interp, "skeleton_index": skeleton_index, "root_index": root_index, "near_list": near_list, "far_list": far_list, "far_count": far_count}


def kernel_block(sources, targets):
    inner_prod = lax.dot_general(sources, targets, (((0,), (0,)), ((), ())), preferred_element_type=jnp.float32)
    source_norm = jnp.sum(jnp.square(sources.astype(jnp.float32)), axis=0)
    target_norm = jnp.sum(jnp.square(targets.astype(jnp.float32)), axis=0)
    return jnp.exp(inner_prod - 0.5 * source_norm[:, None] - 0.5 * target_norm[None, :]).astype(jnp.bfloat16)


def reference(points, charges, leaf_interp, root_interp, skeleton_index, root_index, near_list, far_list, far_count):
    coord_count = points.shape[0]
    leaf_ids = jnp.arange(LEAVES, dtype=jnp.int32)

    def upward(leaf_id):
        weights = lax.dynamic_index_in_dim(charges, leaf_id, 1, keepdims=False)
        matrix = lax.dynamic_index_in_dim(leaf_interp, leaf_id, 0, keepdims=False)
        return lax.dot_general(weights, matrix, (((1,), (1,)), ((), ())), preferred_element_type=jnp.float32).astype(jnp.bfloat16)

    skeleton_weights = lax.map(upward, leaf_ids)
    skeleton_points = jnp.take_along_axis(points, skeleton_index[None, :, :], axis=2)
    grouped_interp = root_interp.reshape(N_LEAF, LEAF_DEV, SKEL, SKEL).astype(jnp.float32)
    grouped_weights = skeleton_weights.reshape(N_LEAF, LEAF_DEV, RHS, SKEL).astype(jnp.float32)
    root_weights = jnp.einsum("oars,oazs->ozr", grouped_interp, grouped_weights, precision=lax.Precision.HIGHEST).astype(jnp.bfloat16)
    owner_points = skeleton_points.reshape(coord_count, N_LEAF, LEAF_DEV * SKEL)
    root_points = jnp.take_along_axis(owner_points, root_index[None, :, :], axis=2)
    all_roots = root_points.reshape(coord_count, N_LEAF * SKEL)
    all_root_weights = jnp.transpose(root_weights, (1, 0, 2)).reshape(RHS, N_LEAF * SKEL)
    column_owner = jnp.arange(N_LEAF * SKEL, dtype=jnp.int32) // SKEL

    def root_one(owner_id):
        target = lax.dynamic_index_in_dim(root_points, owner_id, 1, keepdims=False)
        kernel = kernel_block(all_roots, target)
        distant = jnp.abs(column_owner - owner_id) > 2
        kernel = jnp.where(distant[:, None], kernel, jnp.zeros_like(kernel))
        return jnp.dot(all_root_weights, kernel, preferred_element_type=jnp.float32).astype(jnp.bfloat16)

    root_field = lax.map(root_one, jnp.arange(N_LEAF, dtype=jnp.int32))
    far_slots = jnp.arange(FAR, dtype=jnp.int32)

    def far_one(leaf_id):
        entries = lax.dynamic_index_in_dim(far_list, leaf_id, 0, keepdims=False)
        sources = jnp.take(skeleton_points, entries, axis=1).reshape(coord_count, FAR * SKEL)
        weights = jnp.transpose(jnp.take(skeleton_weights, entries, axis=0), (1, 0, 2)).reshape(RHS, FAR * SKEL)
        target = lax.dynamic_index_in_dim(skeleton_points, leaf_id, 1, keepdims=False)
        kernel = kernel_block(sources, target)
        live_rows = jnp.repeat(far_slots < far_count[leaf_id], SKEL)
        kernel = jnp.where(live_rows[:, None], kernel, jnp.zeros_like(kernel))
        return jnp.dot(weights, kernel, preferred_element_type=jnp.float32)

    far_field = lax.map(far_one, leaf_ids)
    leaf_root = jnp.take(root_field, leaf_ids // LEAF_DEV, axis=0)
    lifted = jnp.einsum("lrs,lzr->lzs", root_interp.astype(jnp.float32), leaf_root.astype(jnp.float32), precision=lax.Precision.HIGHEST)
    skeleton_field = (far_field + lifted).astype(jnp.bfloat16)

    def near_one(leaf_id):
        entries = lax.dynamic_index_in_dim(near_list, leaf_id, 0, keepdims=False)
        sources = jnp.take(points, entries, axis=1).reshape(coord_count, NEAR * LEAF_PTS)
        weights = jnp.take(charges, entries, axis=1).reshape(RHS, NEAR * LEAF_PTS)
        target = lax.dynamic_index_in_dim(points, leaf_id, 1, keepdims=False)
        kernel = kernel_block(sources, target)
        direct = jnp.dot(weights, kernel, preferred_element_type=jnp.float32)
        matrix = lax.dynamic_index_in_dim(leaf_interp, leaf_id, 0, keepdims=False)
        leaf_field = lax.dynamic_index_in_dim(skeleton_field, leaf_id, 0, keepdims=False)
        return direct + jnp.dot(leaf_field, matrix, preferred_element_type=jnp.float32)

    potentials = lax.map(near_one, leaf_ids)
    return jnp.transpose(potentials, (1, 0, 2))
```

```python
import jax
import jax.numpy as jnp
from jax import lax
from jax.experimental import pallas as pl
from jax.experimental.pallas import tpu as pltpu
from jax.sharding import PartitionSpec as P

MESH = pl.DeviceIdType.MESH
F32 = jnp.float32
BF16 = jnp.bfloat16
NT = (((1,), (1,)), ((), ()))

DIM = 64
RHS = 16
RAW = DIM + RHS
ROWS = 96
LEAVES = 16
PTS = 128
BLKS = 4
SKEL = 256
HALO = 8
NEAR = 10
FAR = 32
OWNERS = 64
CHUNKS = 4
CHUNK = LEAVES // CHUNKS
STEPS = (-2, -1, 1, 2)
GROUP = 8
VMEM_LIMIT = 58 * 2**20


def aug_rows(points):
    p = points.astype(F32)
    n = -0.5 * jnp.sum(p * p, axis=0, keepdims=True)
    hi = n.astype(BF16).astype(F32)
    rest = n - hi
    mid = rest.astype(BF16).astype(F32)
    low = rest - mid
    row = lax.broadcasted_iota(jnp.int32, (16, n.shape[1]), 0)
    out = jnp.where(row == 0, hi, jnp.where(row == 1, mid, jnp.where(row == 2, low, 0.0)))
    out = jnp.where((row >= 4) & (row < 7), 1.0, out)
    return out.astype(BF16)


def to_rows(points, aug):
    a = aug.astype(F32)[:8]
    swapped = jnp.concatenate([a[4:], a[:4]], axis=0)
    z16 = jnp.zeros((16, 128), F32)
    z40 = jnp.zeros((40, 128), F32)
    full = jnp.concatenate([points.astype(F32), z16, swapped, z40], axis=0)
    return full.T.astype(BF16)


def leaf_id(z, x, c):
    return (z * 4 + x) * 2 + c


def exchange_kernel(
    own, nl, si, ri, li_hbm, rt_hbm,
    near_o, skel_o, fs_o, wl_o, wr_o, root_o, rts_o,
    gath, halo, srow, swgt, li, rt, fout, fin, rbuf,
    li_sem, rt_sem, y_send, y_recv, f_send, f_recv, h_send, h_recv,
    far_send, far_recv, z_send, z_recv, x_send, x_recv, c_send, c_recv,
):
    o = lax.axis_index("leaf")
    b = lax.axis_index("blk")
    core = lax.rem(o, 2)
    cx = lax.rem(o // 2, 4)
    cz = o // 8
    up = lax.rem(b + 1, BLKS)
    down = lax.rem(b + BLKS - 1, BLKS)
    half = lax.rem(b, 2)
    parity = b // 2
    sender = core == parity

    li_copy = pltpu.make_async_copy(li_hbm, li, li_sem)
    rt_copy = pltpu.make_async_copy(rt_hbm, rt, rt_sem)
    li_copy.start()
    rt_copy.start()

    barrier = pltpu.get_barrier_semaphore()

    def greet(leaf, blk):
        pl.semaphore_signal(barrier, inc=1, device_id=(leaf, blk), device_id_type=MESH)

    greet(o, up)
    greet(o, down)
    for d in range(1, 8):
        greet(leaf_id(lax.rem(cz + d, 8), cx, core), b)
    for d in range(1, 4):
        greet(leaf_id(cz, lax.rem(cx + d, 4), core), b)
    greet(leaf_id(cz, cx, 1 - core), b)
    for step in STEPS:
        @pl.when((o + step >= 0) & (o + step < OWNERS))
        def _():
            greet(o + step, b)
    pl.semaphore_wait(barrier, 13 + jnp.minimum(o, 2) + jnp.minimum(OWNERS - 1 - o, 2))

    def remote(src, dst, ssem, rsem, leaf, blk):
        return pltpu.make_async_remote_copy(
            src_ref=src, dst_ref=dst, send_sem=ssem, recv_sem=rsem,
            device_id=(leaf, blk), device_id_type=MESH)

    has_low = o > 0
    has_high = o < OWNERS - 1
    h_up = remote(own.at[pl.ds(LEAVES - HALO, HALO)], halo.at[0], h_send.at[0], h_recv.at[0], o + 1, b)
    h_down = remote(own.at[pl.ds(0, HALO)], halo.at[1], h_send.at[1], h_recv.at[1], o - 1, b)

    @pl.when(has_high)
    def _():
        h_up.start()

    @pl.when(has_low)
    def _():
        h_down.start()

    def leaves(c):
        return pl.ds(c * CHUNK, CHUNK)

    direct = []
    for c in range(CHUNKS):
        pair = []
        for k, to in enumerate((up, down)):
            pair.append(remote(
                own.at[leaves(c)], gath.at[b, leaves(c), pl.ds(0, RAW)],
                y_send.at[c, k], y_recv.at[c, k], o, to))
        direct.append(pair)
        pair[0].start()
        pair[1].start()

    def forward(c, k):
        src = (down, up)[k]
        to = (up, down)[k]
        part = pl.ds(c * CHUNK + k * (CHUNK // 2), CHUNK // 2)
        ref = gath.at[src, part, pl.ds(0, RAW)]
        return remote(ref, ref, f_send.at[c, k], f_recv.at[c, k], o, to)

    @pl.loop(0, LEAVES)
    def _(l):
        raw = own[l]
        aug = aug_rows(raw[:DIM])
        gath[b, l, 0:RAW, :] = raw
        gath[b, l, RAW:ROWS, :] = aug
        srow[HALO + l] = to_rows(raw[:DIM], aug)
        swgt[HALO + l] = raw[DIM:]

    def take_halo(side, at):
        @pl.loop(0, HALO)
        def _(l):
            raw = halo[side, l]
            srow[at + l] = to_rows(raw[:DIM], aug_rows(raw[:DIM]))
            swgt[at + l] = raw[DIM:]

    def no_halo(at):
        @pl.loop(0, HALO)
        def _(l):
            srow[at + l] = jnp.zeros((128, 128), BF16)
            swgt[at + l] = jnp.zeros((RHS, 128), BF16)

    @pl.when(has_low)
    def _():
        h_up.wait_recv()
        take_halo(0, 0)

    @pl.when(jnp.logical_not(has_low))
    def _():
        no_halo(0)

    @pl.when(has_high)
    def _():
        h_down.wait_recv()
        take_halo(1, HALO + LEAVES)

    @pl.when(jnp.logical_not(has_high))
    def _():
        no_halo(HALO + LEAVES)

    near_base = HALO - o * LEAVES

    def near_leaf(l):
        ids = [jnp.clip(nl[l, j] + near_base, 0, 2 * HALO + LEAVES - 1) for j in range(NEAR)]
        s = jnp.concatenate([srow[i] for i in ids], axis=0)[:, :ROWS]
        w = jnp.concatenate([swgt[i] for i in ids], axis=1)
        t = jnp.concatenate([gath[k, l] for k in range(BLKS)], axis=1)
        x = jnp.dot(s, t, preferred_element_type=F32)
        p = jnp.exp(x).astype(BF16)
        near_o[l] = jnp.dot(w, p, preferred_element_type=F32)

    def near_range(lo, hi):
        @pl.loop(lo, hi)
        def _(l):
            near_leaf(l)

    def skeleton_leaf(l):
        t = jnp.concatenate([gath[k, l] for k in range(BLKS)], axis=1)
        idx = si[pl.ds(l, 1), :]
        m = lax.broadcasted_iota(jnp.int32, (BLKS * PTS, SKEL), 0)
        hot = jnp.where(m == idx, 1.0, 0.0).astype(BF16)
        nat = jnp.dot(t, hot, preferred_element_type=F32)
        wgt = lax.dot_general(t[DIM:RAW], li[l], NT, preferred_element_type=F32)
        skel_o[l] = jnp.concatenate([nat[:DIM], wgt, nat[RAW:]], axis=0).astype(BF16)

    lane = lax.broadcasted_iota(jnp.int32, (ROWS, 128), 1)

    def quarter(l):
        v = skel_o[l].astype(F32)
        return jnp.where(parity == 0, v[:, :128], v[:, 128:])

    def far_pair(q):
        a = quarter(2 * q)
        c = quarter(2 * q + 1)
        a = jnp.where(half == 0, a, pltpu.roll(a, 64, axis=1))
        c = jnp.where(half == 1, c, pltpu.roll(c, 64, axis=1))
        fout[q] = jnp.where(lane < 64, a, c).astype(BF16)

    def far_copy(c, k):
        part = pl.ds(c * 2, 2)
        return remote(fout.at[part], fin.at[3 - k, part], far_send.at[c, k], far_recv.at[c, 3 - k],
                      o + STEPS[k], b)

    def far_wait(c, k):
        part = pl.ds(c * 2, 2)
        return remote(fout.at[part], fin.at[k, part], far_send.at[c, k], far_recv.at[c, k],
                      o + STEPS[k], b)

    li_copy.wait()
    opp = lax.rem(b + 2, BLKS)
    for c in range(CHUNKS):
        direct[c][0].wait_recv()
        forward(c, 0).start()
        direct[c][1].wait_recv()
        forward(c, 1).start()

        @pl.loop(c * CHUNK, (c + 1) * CHUNK)
        def _(l):
            gath[up, l, RAW:ROWS, :] = aug_rows(gath[up, l, 0:DIM, :])
            gath[down, l, RAW:ROWS, :] = aug_rows(gath[down, l, 0:DIM, :])

        forward(c, 0).wait_recv()
        forward(c, 1).wait_recv()

        @pl.loop(c * CHUNK, (c + 1) * CHUNK)
        def _(l):
            gath[opp, l, RAW:ROWS, :] = aug_rows(gath[opp, l, 0:DIM, :])
            skeleton_leaf(l)

        @pl.loop(c * 2, c * 2 + 2)
        def _(q):
            far_pair(q)

        for k, step in enumerate(STEPS):
            @pl.when((o + step >= 0) & (o + step < OWNERS))
            def _():
                far_copy(c, k).start()

        if c < CHUNKS - 1:
            near_range(c * CHUNK, c * CHUNK + 2)

    rt_copy.wait()
    ridx = ri[0:1, :]
    s_id = lax.broadcasted_iota(jnp.int32, (SKEL, SKEL), 0)

    def root_step(l, carry):
        pts, wgt = carry
        hot = jnp.where(s_id + l * SKEL == ridx, 1.0, 0.0).astype(BF16)
        pts = pts + jnp.dot(skel_o[l], hot, preferred_element_type=F32)
        rows = rt[l, pl.ds(pl.multiple_of(half * 128, 128), 128), :]
        wgt = wgt + lax.dot_general(skel_o[l, DIM:RAW, :], rows, NT, preferred_element_type=F32)
        return pts, wgt

    pts, wgt = lax.fori_loop(
        0, LEAVES, root_step, (jnp.zeros((ROWS, SKEL), F32), jnp.zeros((RHS, 128), F32)))
    mine = jnp.where(half == 0, pts[:, :128], pts[:, 128:])

    @pl.when(sender)
    def _():
        rbuf[cx, cz] = jnp.concatenate([mine[:DIM], wgt, mine[RAW:]], axis=0).astype(BF16)

    def root_z(d):
        to = leaf_id(lax.rem(cz + d, 8), cx, core)
        ref = rbuf.at[cx, cz]
        return remote(ref, ref, z_send.at[d - 1], z_recv.at[d - 1], to, b)

    def root_z_wait(d):
        src = lax.rem(cz + 8 - d, 8)
        ref = rbuf.at[cx, src]
        return remote(ref, ref, z_send.at[d - 1], z_recv.at[d - 1], leaf_id(src, cx, core), b)

    def root_x(d):
        to = leaf_id(cz, lax.rem(cx + d, 4), core)
        ref = rbuf.at[cx]
        return remote(ref, ref, x_send.at[d - 1], x_recv.at[d - 1], to, b)

    def root_x_wait(d):
        src = lax.rem(cx + 4 - d, 4)
        ref = rbuf.at[src]
        return remote(ref, ref, x_send.at[d - 1], x_recv.at[d - 1], leaf_id(cz, src, core), b)

    def root_c(d):
        ref = rbuf.at[lax.rem(cx + 4 - d, 4)]
        return remote(ref, ref, c_send.at[d], c_recv.at[d], leaf_id(cz, cx, 1 - core), b)

    @pl.when(sender)
    def _():
        for d in range(1, 8):
            root_z(d).start()

    for h in range(2):
        v = pts[:, h * 128:(h + 1) * 128]
        rts_o[h * 128:(h + 1) * 128, :] = to_rows(v[:DIM], v[RAW:])

    near_range(2, 4)
    near_range(6, 8)

    @pl.when(sender)
    def _():
        for d in range(1, 8):
            root_z_wait(d).wait_recv()
        for d in range(1, 4):
            root_x(d).start()
        root_c(0).start()

    near_range(10, 13)

    @pl.when(sender)
    def _():
        for d in range(1, 4):
            root_x_wait(d).wait_recv()
            root_c(d).start()

    near_range(13, 16)

    wlane = lax.broadcasted_iota(jnp.int32, (RHS, 128), 1)
    for k, step in enumerate(STEPS):
        exists = (o + step >= 0) & (o + step < OWNERS)

        @pl.when(exists)
        def _():
            for c in range(CHUNKS):
                far_wait(c, k).wait_recv()

            @pl.loop(0, 8)
            def _(q):
                v = fin[k, q]
                fs_o[k * 8 + q] = to_rows(v[:DIM], v[RAW:])
                w = v[DIM:RAW].astype(F32)
                left = jnp.where(wlane < 64, w, 0.0)
                right = jnp.where(wlane < 64, 0.0, w)
                even = k * 16 + 2 * q
                wl_o[even] = left.astype(BF16)
                wr_o[even] = pltpu.roll(left, 64, axis=1).astype(BF16)
                wl_o[even + 1] = pltpu.roll(right, 64, axis=1).astype(BF16)
                wr_o[even + 1] = right.astype(BF16)

        @pl.when(jnp.logical_not(exists))
        def _():
            @pl.loop(0, 8)
            def _(q):
                fs_o[k * 8 + q] = jnp.zeros((128, 128), BF16)
                for e in range(2):
                    wl_o[k * 16 + 2 * q + e] = jnp.zeros((RHS, 128), BF16)
                    wr_o[k * 16 + 2 * q + e] = jnp.zeros((RHS, 128), BF16)

    @pl.when(jnp.logical_not(sender))
    def _():
        for d in range(4):
            root_c(d).wait_recv()

    @pl.loop(0, 4)
    def _(x):
        @pl.loop(0, 8)
        def _(z):
            root_o[x * 8 + z] = rbuf[x, z]

    @pl.when(has_high)
    def _():
        h_up.wait_send()

    @pl.when(has_low)
    def _():
        h_down.wait_send()

    for c in range(CHUNKS):
        for k, step in enumerate(STEPS):
            @pl.when((o + step >= 0) & (o + step < OWNERS))
            def _():
                far_copy(c, k).wait_send()
        for k in range(2):
            direct[c][k].wait_send()
            forward(c, k).wait_send()

    @pl.when(sender)
    def _():
        for d in range(1, 8):
            root_z(d).wait_send()
        for d in range(1, 4):
            root_x(d).wait_send()
        for d in range(4):
            root_c(d).wait_send()


def field_kernel(place, table, count, near, skel, fs, wl, wr, root, rts, li_hbm, rt_hbm, part, li, rt, li_sem, rt_sem):
    li_copy = pltpu.make_async_copy(li_hbm, li, li_sem)
    rt_copy = pltpu.make_async_copy(rt_hbm, rt, rt_sem)
    rt_copy.start()
    li_copy.start()
    o = place[0]
    b = place[1]
    parity = b // 2

    targets = rts[:, :ROWS]

    def root_pair(i, acc):
        cols = []
        wgts = []
        for e in range(2):
            k = 2 * i + e
            x = k // 8
            z = k - x * 8
            p = (z * 4 + x) * 2 + parity
            v = root[k]
            cols.append(v)
            wgts.append(jnp.where(jnp.abs(p - o) > 2, v[DIM:RAW].astype(F32), 0.0).astype(BF16))
        xt = jnp.dot(targets, jnp.concatenate(cols, axis=1), preferred_element_type=F32)
        pt = jnp.exp(xt).astype(BF16)
        w = jnp.concatenate(wgts, axis=1)
        return acc + lax.dot_general(w, pt, NT, preferred_element_type=F32)

    rf = lax.fori_loop(0, 16, root_pair, jnp.zeros((RHS, SKEL), F32), unroll=4).astype(BF16)
    rt_copy.wait()
    li_copy.wait()

    @pl.loop(0, LEAVES)
    def _(l):
        n = count[l]
        t = skel[l]

        def group(g, acc):
            ids = [table[l, g * GROUP + j] for j in range(GROUP)]
            s = jnp.concatenate([fs[i] for i in ids], axis=0)[:, :ROWS]
            ws = []
            for j in range(0, GROUP, 2):
                live0 = g * GROUP + j < n
                live1 = g * GROUP + j + 1 < n
                a = jnp.where(live0, wl[ids[j]].astype(F32), 0.0)
                c = jnp.where(live1, wr[ids[j + 1]].astype(F32), 0.0)
                ws.append((a + c).astype(BF16))
            w = jnp.concatenate(ws, axis=1)
            x = jnp.dot(s, t, preferred_element_type=F32)
            p = jnp.exp(x).astype(BF16)
            return acc + jnp.dot(w, p, preferred_element_type=F32)

        acc = jnp.dot(rf, rt[l], preferred_element_type=F32)
        acc = lax.fori_loop(0, (n + GROUP - 1) // GROUP, group, acc)
        out = near[l] + jnp.dot(acc.astype(BF16), li[l], preferred_element_type=F32)
        out = out.astype(BF16)
        for d in range(BLKS):
            part[d, l] = out[:, d * 128:(d + 1) * 128]


def scatter_kernel(part, out, land, send, recv):
    o = lax.axis_index("leaf")
    b = lax.axis_index("blk")
    barrier = pltpu.get_barrier_semaphore()
    for d in range(1, BLKS):
        pl.semaphore_signal(barrier, inc=1, device_id=(o, lax.rem(b + d, BLKS)), device_id_type=MESH)
    pl.semaphore_wait(barrier, BLKS - 1)
    copies = []
    for d in (2, 1, 3):
        to = lax.rem(b + d, BLKS)
        copy = pltpu.make_async_remote_copy(
            src_ref=part.at[to], dst_ref=land.at[d - 1], send_sem=send.at[d - 1],
            recv_sem=recv.at[d - 1], device_id=(o, to), device_id_type=MESH)
        copy.start()
        copies.append(copy)
    for copy in copies:
        copy.wait_recv()
    for l in range(LEAVES):
        total = part[b, l].astype(F32)
        for d in range(BLKS - 1):
            total = total + land[d, l].astype(F32)
        out[:, l, :] = total
    for copy in copies:
        copy.wait_send()


def on_device(points, charges, leaf_interp, root_interp, skeleton_index, root_index, near_list, far_list, far_count):
    o = lax.axis_index("leaf").astype(jnp.int32)
    b = lax.axis_index("blk").astype(jnp.int32)
    own = jnp.transpose(jnp.concatenate([points, charges], axis=0), (1, 0, 2))
    vmem = pl.BlockSpec(memory_space=pltpu.VMEM)
    smem = pl.BlockSpec(memory_space=pltpu.SMEM)
    hbm = pl.BlockSpec(memory_space=pl.ANY)
    dma = pltpu.SemaphoreType.DMA

    near, skel, fs, wl, wr, root, rts = pl.pallas_call(
        exchange_kernel,
        out_shape=(
            jax.ShapeDtypeStruct((LEAVES, RHS, BLKS * PTS), F32),
            jax.ShapeDtypeStruct((LEAVES, ROWS, SKEL), BF16),
            jax.ShapeDtypeStruct((32, 128, 128), BF16),
            jax.ShapeDtypeStruct((64, RHS, 128), BF16),
            jax.ShapeDtypeStruct((64, RHS, 128), BF16),
            jax.ShapeDtypeStruct((32, ROWS, 128), BF16),
            jax.ShapeDtypeStruct((SKEL, 128), BF16),
        ),
        in_specs=[vmem, smem, vmem, vmem, hbm, hbm],
        out_specs=(vmem,) * 7,
        scratch_shapes=[
            pltpu.VMEM((BLKS, LEAVES, ROWS, PTS), BF16),
            pltpu.VMEM((2, HALO, RAW, PTS), BF16),
            pltpu.VMEM((2 * HALO + LEAVES, 128, 128), BF16),
            pltpu.VMEM((2 * HALO + LEAVES, RHS, 128), BF16),
            pltpu.VMEM((LEAVES, SKEL, BLKS * PTS), BF16),
            pltpu.VMEM((LEAVES, SKEL, SKEL), BF16),
            pltpu.VMEM((8, ROWS, 128), BF16),
            pltpu.VMEM((4, 8, ROWS, 128), BF16),
            pltpu.VMEM((4, 8, ROWS, 128), BF16),
            dma, dma,
            dma((CHUNKS, 2)), dma((CHUNKS, 2)), dma((CHUNKS, 2)), dma((CHUNKS, 2)),
            dma((2,)), dma((2,)),
            dma((CHUNKS, 4)), dma((CHUNKS, 4)),
            dma((7,)), dma((7,)), dma((3,)), dma((3,)), dma((4,)), dma((4,)),
        ],
        compiler_params=pltpu.CompilerParams(
            collective_id=0, has_side_effects=True, vmem_limit_bytes=VMEM_LIMIT),
    )(own, near_list, skeleton_index, root_index, leaf_interp, root_interp)

    source_owner = far_list // LEAVES
    offset = source_owner - o
    table = (offset + 2 - (offset > 0).astype(jnp.int32)) * LEAVES + far_list - source_owner * LEAVES
    live = jnp.arange(FAR, dtype=jnp.int32)[None, :] < far_count[:, None]
    table = jnp.clip(jnp.where(live, table, table[:, :1]), 0, 63)
    place = jnp.stack([o, b])

    part = pl.pallas_call(
        field_kernel,
        out_shape=jax.ShapeDtypeStruct((BLKS, LEAVES, RHS, PTS), BF16),
        in_specs=[smem, smem, smem, vmem, vmem, vmem, vmem, vmem, vmem, vmem, hbm, hbm],
        out_specs=vmem,
        scratch_shapes=[
            pltpu.VMEM((LEAVES, SKEL, BLKS * PTS), BF16),
            pltpu.VMEM((LEAVES, SKEL, SKEL), BF16),
            dma, dma,
        ],
        compiler_params=pltpu.CompilerParams(vmem_limit_bytes=VMEM_LIMIT),
    )(place, table, far_count, near, skel, fs.reshape(64, 64, 128), wl, wr, root, rts, leaf_interp, root_interp)

    return pl.pallas_call(
        scatter_kernel,
        out_shape=jax.ShapeDtypeStruct((RHS, LEAVES, PTS), F32),
        in_specs=[vmem],
        out_specs=vmem,
        scratch_shapes=[
            pltpu.VMEM((BLKS - 1, LEAVES, RHS, PTS), BF16),
            dma((BLKS - 1,)), dma((BLKS - 1,)),
        ],
        compiler_params=pltpu.CompilerParams(
            collective_id=1, has_side_effects=True, vmem_limit_bytes=VMEM_LIMIT),
    )(part)


def solution(mesh):
    placed = (
        P(None, "leaf", "blk"),
        P(None, "leaf", "blk"),
        P("leaf", None, None),
        P("leaf", None, None),
        P("leaf", None),
        P("leaf", None),
        P("leaf", None),
        P("leaf", None),
        P("leaf"),
    )
    return jax.shard_map(
        on_device, mesh=mesh, in_specs=placed, out_specs=P(None, "leaf", "blk"), check_vma=False
    )
```

```python
import jax
import jax.numpy as jnp
from jax import lax
from jax.experimental import pallas as pl
from jax.experimental.pallas import tpu as pltpu
from jax.sharding import PartitionSpec as P

MESH = pl.DeviceIdType.MESH
F32 = jnp.float32
BF16 = jnp.bfloat16
NT = (((1,), (1,)), ((), ()))

DIM = 64
RHS = 16
RAW = DIM + RHS
ROWS = 96
LEAVES = 16
PTS = 128
BLKS = 4
SKEL = 256
HALO = 8
NEAR = 10
FAR = 32
OWNERS = 64
CHUNKS = 4
CHUNK = LEAVES // CHUNKS
AHEAD = 2
STEPS = (-2, -1, 1, 2)
PAIRS = FAR // 2
VMEM_LIMIT = 58 * 2**20


def aug_rows(points):
    p = points.astype(F32)
    n = -0.5 * jnp.sum(p * p, axis=0, keepdims=True)
    hi = n.astype(BF16).astype(F32)
    rest = n - hi
    mid = rest.astype(BF16).astype(F32)
    low = rest - mid
    row = lax.broadcasted_iota(jnp.int32, (16, n.shape[1]), 0)
    out = jnp.where(row == 0, hi, jnp.where(row == 1, mid, jnp.where(row == 2, low, 0.0)))
    out = jnp.where((row >= 4) & (row < 7), 1.0, out)
    return out.astype(BF16)


def to_rows(points, aug):
    a = aug.astype(F32)[:8]
    swapped = jnp.concatenate([a[4:], a[:4]], axis=0)
    z16 = jnp.zeros((16, 128), F32)
    z40 = jnp.zeros((40, 128), F32)
    full = jnp.concatenate([points.astype(F32), z16, swapped, z40], axis=0)
    return full.T.astype(BF16)


def leaf_id(z, x, c):
    return (z * 4 + x) * 2 + c


def potential_kernel(
    own, nl, fl_s, fl_v, si, ri, li_hbm, rt_hbm,
    out,
    gath, halo, srow, swgt, li, rt, fout, fin, rbuf,
    near_o, skel_o, fs, wl, wr, rts, sall, wall, mask, farsum, part, land,
    li_sem, rt_sem, y_send, y_recv, f_send, f_recv, h_send, h_recv,
    far_send, far_recv, z_send, z_recv, x_send, x_recv, c_send, c_recv, s_send, s_recv,
):
    o = lax.axis_index("leaf")
    b = lax.axis_index("blk")
    core = lax.rem(o, 2)
    cx = lax.rem(o // 2, 4)
    cz = o // 8
    up = lax.rem(b + 1, BLKS)
    down = lax.rem(b + BLKS - 1, BLKS)
    half = lax.rem(b, 2)
    parity = b // 2
    sender = core == parity

    li_copy = pltpu.make_async_copy(li_hbm, li, li_sem)
    rt_copy = pltpu.make_async_copy(rt_hbm, rt, rt_sem)
    li_copy.start()
    rt_copy.start()

    barrier = pltpu.get_barrier_semaphore()

    def greet(leaf, blk):
        pl.semaphore_signal(barrier, inc=1, device_id=(leaf, blk), device_id_type=MESH)

    greet(o, up)
    greet(o, down)
    for d in range(1, 8):
        greet(leaf_id(lax.rem(cz + d, 8), cx, core), b)
    for d in range(1, 4):
        greet(leaf_id(cz, lax.rem(cx + d, 4), core), b)
    greet(leaf_id(cz, cx, 1 - core), b)
    greet(o, lax.rem(b + 2, BLKS))
    for step in STEPS:
        @pl.when((o + step >= 0) & (o + step < OWNERS))
        def _():
            greet(o + step, b)
    pl.semaphore_wait(barrier, 14 + jnp.minimum(o, 2) + jnp.minimum(OWNERS - 1 - o, 2))

    def remote(src, dst, ssem, rsem, leaf, blk):
        return pltpu.make_async_remote_copy(
            src_ref=src, dst_ref=dst, send_sem=ssem, recv_sem=rsem,
            device_id=(leaf, blk), device_id_type=MESH)

    has_low = o > 0
    has_high = o < OWNERS - 1
    h_up = remote(own.at[pl.ds(LEAVES - HALO, HALO)], halo.at[0], h_send.at[0], h_recv.at[0], o + 1, b)
    h_down = remote(own.at[pl.ds(0, HALO)], halo.at[1], h_send.at[1], h_recv.at[1], o - 1, b)

    @pl.when(has_high)
    def _():
        h_up.start()

    @pl.when(has_low)
    def _():
        h_down.start()

    def leaves(c):
        return pl.ds(c * CHUNK, CHUNK)

    direct = []
    for c in range(CHUNKS):
        pair = []
        for k, to in enumerate((up, down)):
            pair.append(remote(
                own.at[leaves(c)], gath.at[b, leaves(c), pl.ds(0, RAW)],
                y_send.at[c, k], y_recv.at[c, k], o, to))
        direct.append(pair)
        if c < AHEAD:
            pair[0].start()
            pair[1].start()

    def forward(c, k):
        src = (down, up)[k]
        to = (up, down)[k]
        part = pl.ds(c * CHUNK + k * (CHUNK // 2), CHUNK // 2)
        ref = gath.at[src, part, pl.ds(0, RAW)]
        return remote(ref, ref, f_send.at[c, k], f_recv.at[c, k], o, to)

    @pl.loop(0, LEAVES)
    def _(l):
        raw = own[l]
        aug = aug_rows(raw[:DIM])
        gath[b, l, 0:RAW, :] = raw
        gath[b, l, RAW:ROWS, :] = aug
        srow[HALO + l] = to_rows(raw[:DIM], aug)
        swgt[HALO + l] = raw[DIM:]

    def take_halo(side, at):
        @pl.loop(0, HALO)
        def _(l):
            raw = halo[side, l]
            srow[at + l] = to_rows(raw[:DIM], aug_rows(raw[:DIM]))
            swgt[at + l] = raw[DIM:]

    def no_halo(at):
        @pl.loop(0, HALO)
        def _(l):
            srow[at + l] = jnp.zeros((128, 128), BF16)
            swgt[at + l] = jnp.zeros((RHS, 128), BF16)

    @pl.when(has_low)
    def _():
        h_up.wait_recv()
        take_halo(0, 0)

    @pl.when(jnp.logical_not(has_low))
    def _():
        no_halo(0)

    @pl.when(has_high)
    def _():
        h_down.wait_recv()
        take_halo(1, HALO + LEAVES)

    @pl.when(jnp.logical_not(has_high))
    def _():
        no_halo(HALO + LEAVES)

    near_base = HALO - o * LEAVES

    def near_leaf(l):
        ids = [jnp.clip(nl[l, j] + near_base, 0, 2 * HALO + LEAVES - 1) for j in range(NEAR)]
        s = jnp.concatenate([srow[i] for i in ids], axis=0)[:, :ROWS]
        w = jnp.concatenate([swgt[i] for i in ids], axis=1)
        t = jnp.concatenate([gath[k, l] for k in range(BLKS)], axis=1)
        x = jnp.dot(s, t, preferred_element_type=F32)
        p = jnp.exp(x).astype(BF16)
        near_o[l] = jnp.dot(w, p, preferred_element_type=F32)

    def near_range(lo, hi):
        @pl.loop(lo, hi)
        def _(l):
            near_leaf(l)

    def skeleton_leaf(l):
        t = jnp.concatenate([gath[k, l] for k in range(BLKS)], axis=1)
        idx = si[pl.ds(l, 1), :]
        m = lax.broadcasted_iota(jnp.int32, (BLKS * PTS, SKEL), 0)
        hot = jnp.where(m == idx, 1.0, 0.0).astype(BF16)
        nat = jnp.dot(t, hot, preferred_element_type=F32)
        wgt = lax.dot_general(t[DIM:RAW], li[l], NT, preferred_element_type=F32)
        skel_o[l] = jnp.concatenate([nat[:DIM], wgt, nat[RAW:]], axis=0).astype(BF16)

    lane = lax.broadcasted_iota(jnp.int32, (ROWS, 128), 1)

    def quarter(l):
        v = skel_o[l].astype(F32)
        return jnp.where(parity == 0, v[:, :128], v[:, 128:])

    def far_pair(q):
        a = quarter(2 * q)
        c = quarter(2 * q + 1)
        a = jnp.where(half == 0, a, pltpu.roll(a, 64, axis=1))
        c = jnp.where(half == 1, c, pltpu.roll(c, 64, axis=1))
        fout[q] = jnp.where(lane < 64, a, c).astype(BF16)

    def far_copy(c, k):
        part = pl.ds(c * 2, 2)
        return remote(fout.at[part], fin.at[3 - k, part], far_send.at[c, k], far_recv.at[c, 3 - k],
                      o + STEPS[k], b)

    def far_wait(c, k):
        part = pl.ds(c * 2, 2)
        return remote(fout.at[part], fin.at[k, part], far_send.at[c, k], far_recv.at[c, k],
                      o + STEPS[k], b)

    li_copy.wait()
    opp = lax.rem(b + 2, BLKS)

    def chunk_work(c):
        @pl.loop(c * CHUNK, (c + 1) * CHUNK)
        def _(l):
            gath[up, l, RAW:ROWS, :] = aug_rows(gath[up, l, 0:DIM, :])
            gath[down, l, RAW:ROWS, :] = aug_rows(gath[down, l, 0:DIM, :])

        forward(c, 0).wait_recv()
        forward(c, 1).wait_recv()

        @pl.loop(c * CHUNK, (c + 1) * CHUNK, unroll=2)
        def _(l):
            gath[opp, l, RAW:ROWS, :] = aug_rows(gath[opp, l, 0:DIM, :])
            skeleton_leaf(l)

        @pl.loop(c * 2, c * 2 + 2)
        def _(q):
            far_pair(q)

        for k, step in enumerate(STEPS):
            @pl.when((o + step >= 0) & (o + step < OWNERS))
            def _():
                far_copy(c, k).start()

    for c in range(CHUNKS):
        direct[c][0].wait_recv()
        forward(c, 0).start()
        direct[c][1].wait_recv()
        forward(c, 1).start()
        if c + AHEAD < CHUNKS:
            direct[c + AHEAD][0].start()
            direct[c + AHEAD][1].start()
        if c > 0:
            chunk_work(c - 1)
            near_range((c - 1) * CHUNK, (c - 1) * CHUNK + 2)
    chunk_work(CHUNKS - 1)

    rt_copy.wait()
    ridx = ri[0:1, :]
    s_id = lax.broadcasted_iota(jnp.int32, (SKEL, SKEL), 0)

    def root_step(l, carry):
        pts, wgt = carry
        hot = jnp.where(s_id + l * SKEL == ridx, 1.0, 0.0).astype(BF16)
        pts = pts + jnp.dot(skel_o[l], hot, preferred_element_type=F32)
        rows = rt[l, pl.ds(pl.multiple_of(half * 128, 128), 128), :]
        wgt = wgt + lax.dot_general(skel_o[l, DIM:RAW, :], rows, NT, preferred_element_type=F32)
        return pts, wgt

    pts, wgt = lax.fori_loop(
        0, LEAVES, root_step, (jnp.zeros((ROWS, SKEL), F32), jnp.zeros((RHS, 128), F32)))
    mine = jnp.where(half == 0, pts[:, :128], pts[:, 128:])

    @pl.when(sender)
    def _():
        rbuf[cx, cz] = jnp.concatenate([mine[:DIM], wgt, mine[RAW:]], axis=0).astype(BF16)

    def root_z(d):
        to = leaf_id(lax.rem(cz + d, 8), cx, core)
        ref = rbuf.at[cx, cz]
        return remote(ref, ref, z_send.at[d - 1], z_recv.at[d - 1], to, b)

    def root_z_wait(d):
        src = lax.rem(cz + 8 - d, 8)
        ref = rbuf.at[cx, src]
        return remote(ref, ref, z_send.at[d - 1], z_recv.at[d - 1], leaf_id(src, cx, core), b)

    def root_x(d):
        to = leaf_id(cz, lax.rem(cx + d, 4), core)
        ref = rbuf.at[cx]
        return remote(ref, ref, x_send.at[d - 1], x_recv.at[d - 1], to, b)

    def root_x_wait(d):
        src = lax.rem(cx + 4 - d, 4)
        ref = rbuf.at[src]
        return remote(ref, ref, x_send.at[d - 1], x_recv.at[d - 1], leaf_id(cz, src, core), b)

    def root_c(d):
        ref = rbuf.at[lax.rem(cx + 4 - d, 4)]
        return remote(ref, ref, c_send.at[d], c_recv.at[d], leaf_id(cz, cx, 1 - core), b)

    @pl.when(sender)
    def _():
        for d in range(1, 8):
            root_z(d).start()

    for h in range(2):
        v = pts[:, h * 128:(h + 1) * 128]
        rts[h * 128:(h + 1) * 128, :] = to_rows(v[:DIM], v[RAW:])

    near_range(2, 4)
    near_range(6, 8)
    near_range(10, 12)

    @pl.when(sender)
    def _():
        for d in range(1, 8):
            root_z_wait(d).wait_recv()
        for d in range(1, 4):
            root_x(d).start()
        root_c(0).start()

    near_range(12, 16)

    wlane = lax.broadcasted_iota(jnp.int32, (RHS, 128), 1)
    for k, step in enumerate(STEPS):
        exists = (o + step >= 0) & (o + step < OWNERS)

        @pl.when(exists)
        def _():
            for c in range(CHUNKS):
                far_wait(c, k).wait_recv()

            @pl.loop(0, 8)
            def _(q):
                v = fin[k, q]
                even = k * 16 + 2 * q
                rows = to_rows(v[:DIM], v[RAW:])
                fs[even] = rows[:64]
                fs[even + 1] = rows[64:]
                w = v[DIM:RAW].astype(F32)
                left = jnp.where(wlane < 64, w, 0.0)
                right = jnp.where(wlane < 64, 0.0, w)
                wl[even] = left
                wr[even] = pltpu.roll(left, 64, axis=1)
                wl[even + 1] = pltpu.roll(right, 64, axis=1)
                wr[even + 1] = right

        @pl.when(jnp.logical_not(exists))
        def _():
            @pl.loop(k * 16, k * 16 + 16)
            def _(e):
                fs[e] = jnp.zeros((64, 128), BF16)
                wl[e] = jnp.zeros((RHS, 128), F32)
                wr[e] = jnp.zeros((RHS, 128), F32)

    lists = fl_v[...]

    def named(u):
        f = fl_s[0, u]
        owner = f // LEAVES
        step = owner - o
        at = (step + 2 - jnp.where(step > 0, 1, 0)) * LEAVES + f - owner * LEAVES
        hit = jnp.max(jnp.where(lists == f, 1.0, 0.0), axis=1, keepdims=True)
        return jnp.clip(at, 0, 63), hit * jnp.where(step == 0, 0.0, 1.0)

    for v in range(PAIRS):
        at0, hit0 = named(2 * v)
        at1, hit1 = named(2 * v + 1)
        sall[v * 128:v * 128 + 64, :] = fs[at0]
        sall[v * 128 + 64:v * 128 + 128, :] = fs[at1]
        wall[:, v * 128:(v + 1) * 128] = wl[at0] + wr[at1]
        mask[:, v * 128:(v + 1) * 128] = jnp.where(wlane < 64, hit0, hit1)

    def far_range(lo, hi):
        @pl.loop(lo, hi, step=2)
        def _(l):
            t = jnp.concatenate([skel_o[l], skel_o[l + 1]], axis=1)
            w0 = (wall[...] * mask[pl.ds(l, 1), :]).astype(BF16)
            w1 = (wall[...] * mask[pl.ds(l + 1, 1), :]).astype(BF16)
            x = jnp.dot(sall[:, :ROWS], t, preferred_element_type=F32)
            p = jnp.exp(x).astype(BF16)
            farsum[l] = jnp.dot(w0, p[:, :SKEL], preferred_element_type=F32)
            farsum[l + 1] = jnp.dot(w1, p[:, SKEL:], preferred_element_type=F32)

    far_range(0, 6)

    @pl.when(sender)
    def _():
        for d in range(1, 4):
            root_x_wait(d).wait_recv()
            root_c(d).start()

    far_range(6, 16)

    @pl.when(jnp.logical_not(sender))
    def _():
        for d in range(4):
            root_c(d).wait_recv()

    targets = rts[:, :ROWS]

    def root_group(i, acc):
        cols = []
        wgts = []
        for e in range(4):
            x = i // 2
            z = (i - 2 * x) * 4 + e
            p = leaf_id(z, x, parity)
            v = rbuf[x, z]
            cols.append(v)
            wgts.append(jnp.where(jnp.abs(p - o) > 2, v[DIM:RAW].astype(F32), 0.0).astype(BF16))
        xt = jnp.dot(targets, jnp.concatenate(cols, axis=1), preferred_element_type=F32)
        pt = jnp.exp(xt).astype(BF16)
        w = jnp.concatenate(wgts, axis=1)
        return acc + lax.dot_general(w, pt, NT, preferred_element_type=F32)

    rf = lax.fori_loop(0, 8, root_group, jnp.zeros((RHS, SKEL), F32), unroll=2).astype(BF16)

    def scatter_copy(c, d):
        to = lax.rem(b + d, BLKS)
        return remote(part.at[to, leaves(c)], land.at[d - 1, leaves(c)],
                      s_send.at[c, d - 1], s_recv.at[c, d - 1], o, to)

    for c in range(CHUNKS):
        group = range(c * CHUNK, (c + 1) * CHUNK)
        fields = [
            (farsum[l] + jnp.dot(rf, rt[l], preferred_element_type=F32)).astype(BF16) for l in group
        ]
        for l, field in zip(group, fields):
            total = near_o[l] + jnp.dot(field, li[l], preferred_element_type=F32)
            total = total.astype(BF16)
            for d in range(BLKS):
                part[d, l] = total[:, d * 128:(d + 1) * 128]
        for d in (2, 1, 3):
            scatter_copy(c, d).start()

    for c in range(CHUNKS):
        for d in (1, 2, 3):
            scatter_copy(c, d).wait_recv()
        for l in range(c * CHUNK, (c + 1) * CHUNK):
            total = part[b, l].astype(F32)
            for d in range(BLKS - 1):
                total = total + land[d, l].astype(F32)
            out[l] = total

    @pl.when(has_high)
    def _():
        h_up.wait_send()

    @pl.when(has_low)
    def _():
        h_down.wait_send()

    for c in range(CHUNKS):
        for k, step in enumerate(STEPS):
            @pl.when((o + step >= 0) & (o + step < OWNERS))
            def _():
                far_copy(c, k).wait_send()
        for d in (1, 2, 3):
            scatter_copy(c, d).wait_send()
        for k in range(2):
            direct[c][k].wait_send()
            forward(c, k).wait_send()

    @pl.when(sender)
    def _():
        for d in range(1, 8):
            root_z(d).wait_send()
        for d in range(1, 4):
            root_x(d).wait_send()
        for d in range(4):
            root_c(d).wait_send()


def on_device(points, charges, leaf_interp, root_interp, skeleton_index, root_index, near_list, far_list, far_count):
    own = jnp.transpose(jnp.concatenate([points, charges], axis=0), (1, 0, 2))
    vmem = pl.BlockSpec(memory_space=pltpu.VMEM)
    smem = pl.BlockSpec(memory_space=pltpu.SMEM)
    hbm = pl.BlockSpec(memory_space=pl.ANY)
    dma = pltpu.SemaphoreType.DMA

    out = pl.pallas_call(
        potential_kernel,
        out_shape=jax.ShapeDtypeStruct((LEAVES, RHS, PTS), F32),
        in_specs=[vmem, smem, smem, vmem, vmem, vmem, hbm, hbm],
        out_specs=vmem,
        scratch_shapes=[
            pltpu.VMEM((BLKS, LEAVES, ROWS, PTS), BF16),
            pltpu.VMEM((2, HALO, RAW, PTS), BF16),
            pltpu.VMEM((2 * HALO + LEAVES, 128, 128), BF16),
            pltpu.VMEM((2 * HALO + LEAVES, RHS, 128), BF16),
            pltpu.VMEM((LEAVES, SKEL, BLKS * PTS), BF16),
            pltpu.VMEM((LEAVES, SKEL, SKEL), BF16),
            pltpu.VMEM((8, ROWS, 128), BF16),
            pltpu.VMEM((4, 8, ROWS, 128), BF16),
            pltpu.VMEM((4, 8, ROWS, 128), BF16),
            pltpu.VMEM((LEAVES, RHS, BLKS * PTS), F32),
            pltpu.VMEM((LEAVES, ROWS, SKEL), BF16),
            pltpu.VMEM((64, 64, 128), BF16),
            pltpu.VMEM((64, RHS, 128), F32),
            pltpu.VMEM((64, RHS, 128), F32),
            pltpu.VMEM((SKEL, 128), BF16),
            pltpu.VMEM((PAIRS * 128, 128), BF16),
            pltpu.VMEM((RHS, PAIRS * 128), F32),
            pltpu.VMEM((LEAVES, PAIRS * 128), F32),
            pltpu.VMEM((LEAVES, RHS, SKEL), F32),
            pltpu.VMEM((BLKS, LEAVES, RHS, PTS), BF16),
            pltpu.VMEM((BLKS - 1, LEAVES, RHS, PTS), BF16),
            dma, dma,
            dma((CHUNKS, 2)), dma((CHUNKS, 2)), dma((CHUNKS, 2)), dma((CHUNKS, 2)),
            dma((2,)), dma((2,)),
            dma((CHUNKS, 4)), dma((CHUNKS, 4)),
            dma((7,)), dma((7,)), dma((3,)), dma((3,)), dma((4,)), dma((4,)),
            dma((CHUNKS, 3)), dma((CHUNKS, 3)),
        ],
        compiler_params=pltpu.CompilerParams(
            collective_id=0, has_side_effects=True, vmem_limit_bytes=VMEM_LIMIT),
    )(own, near_list, far_list, far_list, skeleton_index, root_index, leaf_interp, root_interp)
    return jnp.transpose(out, (1, 0, 2))


def solution(mesh):
    placed = (
        P(None, "leaf", "blk"),
        P(None, "leaf", "blk"),
        P("leaf", None, None),
        P("leaf", None, None),
        P("leaf", None),
        P("leaf", None),
        P("leaf", None),
        P("leaf", None),
        P("leaf"),
    )
    return jax.shard_map(
        on_device, mesh=mesh, in_specs=placed, out_specs=P(None, "leaf", "blk"), check_vma=False
    )
```

```python
import jax
import jax.numpy as jnp
from jax import lax
from jax.experimental import pallas as pl
from jax.experimental.pallas import tpu as pltpu
from jax.sharding import PartitionSpec as P

MESH = pl.DeviceIdType.MESH
F32 = jnp.float32
BF16 = jnp.bfloat16
NT = (((1,), (1,)), ((), ()))

DIM = 64
RHS = 16
RAW = DIM + RHS
ROWS = 96
LEAVES = 16
PTS = 128
BLKS = 4
SKEL = 256
HALO = 8
NEAR = 10
FAR = 32
OWNERS = 64
CHUNKS = 4
CHUNK = LEAVES // CHUNKS
AHEAD = 3
STEPS = (-2, -1, 1, 2)
PAIRS = FAR // 2
VMEM_LIMIT = 58 * 2**20


def aug_rows(points):
    p = points.astype(F32)
    n = -0.5 * jnp.sum(p * p, axis=0, keepdims=True)
    hi = n.astype(BF16).astype(F32)
    rest = n - hi
    mid = rest.astype(BF16).astype(F32)
    low = rest - mid
    row = lax.broadcasted_iota(jnp.int32, (16, n.shape[1]), 0)
    out = jnp.where(row == 0, hi, jnp.where(row == 1, mid, jnp.where(row == 2, low, 0.0)))
    out = jnp.where((row >= 4) & (row < 7), 1.0, out)
    return out.astype(BF16)


def to_rows(points, aug):
    a = aug.astype(F32)[:8]
    swapped = jnp.concatenate([a[4:], a[:4]], axis=0)
    z16 = jnp.zeros((16, 128), F32)
    z40 = jnp.zeros((40, 128), F32)
    full = jnp.concatenate([points.astype(F32), z16, swapped, z40], axis=0)
    return full.T.astype(BF16)


def leaf_id(z, x, c):
    return (z * 4 + x) * 2 + c


def potential_kernel(
    points, charges, nl, fl_s, fl_v, si, ri, li_hbm, rt_hbm,
    out,
    own, gath, halo, srow, swgt, li, rt, fout, fin, rbuf,
    near_o, skel_o, fs, wl, wr, rts, sall, wall, mask, farsum, part, land, rfs,
    li_sem, rt_sem, y_send, y_recv, f_send, f_recv, h_send, h_recv,
    far_send, far_recv, z_send, z_recv, x_send, x_recv, c_send, c_recv, s_send, s_recv, r_send, r_recv,
):
    o = lax.axis_index("leaf")
    b = lax.axis_index("blk")
    core = lax.rem(o, 2)
    cx = lax.rem(o // 2, 4)
    cz = o // 8
    up = lax.rem(b + 1, BLKS)
    down = lax.rem(b + BLKS - 1, BLKS)
    half = lax.rem(b, 2)
    parity = b // 2
    sender = core == parity

    li_copy = pltpu.make_async_copy(li_hbm, li, li_sem)
    rt_copy = pltpu.make_async_copy(rt_hbm, rt, rt_sem)
    li_copy.start()
    rt_copy.start()

    barrier = pltpu.get_barrier_semaphore()

    def greet(leaf, blk):
        pl.semaphore_signal(barrier, inc=1, device_id=(leaf, blk), device_id_type=MESH)

    greet(o, up)
    greet(o, down)
    for d in range(1, 8):
        greet(leaf_id(lax.rem(cz + d, 8), cx, core), b)
    for d in range(1, 4):
        greet(leaf_id(cz, lax.rem(cx + d, 4), core), b)
    greet(leaf_id(cz, cx, 1 - core), b)
    greet(o, lax.rem(b + 2, BLKS))
    for step in STEPS:
        @pl.when((o + step >= 0) & (o + step < OWNERS))
        def _():
            greet(o + step, b)

    for h in range(2):
        for g in range(DIM // 16):
            v = points[g * 16:(g + 1) * 16, h * 8:(h + 1) * 8, :].astype(F32)
            own[h * 8:(h + 1) * 8, g * 16:(g + 1) * 16, :] = jnp.swapaxes(v, 0, 1).astype(BF16)
        v = charges[:, h * 8:(h + 1) * 8, :].astype(F32)
        own[h * 8:(h + 1) * 8, DIM:RAW, :] = jnp.swapaxes(v, 0, 1).astype(BF16)

    @pl.loop(0, LEAVES, unroll=2)
    def _(l):
        raw = own[l]
        aug = aug_rows(raw[:DIM])
        gath[b, l, 0:RAW, :] = raw
        gath[b, l, RAW:ROWS, :] = aug
        srow[HALO + l] = to_rows(raw[:DIM], aug)
        swgt[HALO + l] = raw[DIM:]

    pl.semaphore_wait(barrier, 14 + jnp.minimum(o, 2) + jnp.minimum(OWNERS - 1 - o, 2))

    def remote(src, dst, ssem, rsem, leaf, blk):
        return pltpu.make_async_remote_copy(
            src_ref=src, dst_ref=dst, send_sem=ssem, recv_sem=rsem,
            device_id=(leaf, blk), device_id_type=MESH)

    has_low = o > 0
    has_high = o < OWNERS - 1
    h_up = remote(own.at[pl.ds(LEAVES - HALO, HALO)], halo.at[0], h_send.at[0], h_recv.at[0], o + 1, b)
    h_down = remote(own.at[pl.ds(0, HALO)], halo.at[1], h_send.at[1], h_recv.at[1], o - 1, b)

    @pl.when(has_high)
    def _():
        h_up.start()

    @pl.when(has_low)
    def _():
        h_down.start()

    def leaves(c):
        return pl.ds(c * CHUNK, CHUNK)

    direct = []
    for c in range(CHUNKS):
        pair = []
        for k, to in enumerate((up, down)):
            pair.append(remote(
                own.at[leaves(c)], gath.at[b, leaves(c), pl.ds(0, RAW)],
                y_send.at[c, k], y_recv.at[c, k], o, to))
        direct.append(pair)
        if c < AHEAD:
            pair[0].start()
            pair[1].start()

    def forward(c, k):
        src = (down, up)[k]
        to = (up, down)[k]
        part = pl.ds(c * CHUNK + k * (CHUNK // 2), CHUNK // 2)
        ref = gath.at[src, part, pl.ds(0, RAW)]
        return remote(ref, ref, f_send.at[c, k], f_recv.at[c, k], o, to)

    def take_halo(side, at):
        @pl.loop(0, HALO)
        def _(l):
            raw = halo[side, l]
            srow[at + l] = to_rows(raw[:DIM], aug_rows(raw[:DIM]))
            swgt[at + l] = raw[DIM:]

    def no_halo(at):
        @pl.loop(0, HALO)
        def _(l):
            srow[at + l] = jnp.zeros((128, 128), BF16)
            swgt[at + l] = jnp.zeros((RHS, 128), BF16)

    @pl.when(has_low)
    def _():
        h_up.wait_recv()
        take_halo(0, 0)

    @pl.when(jnp.logical_not(has_low))
    def _():
        no_halo(0)

    @pl.when(has_high)
    def _():
        h_down.wait_recv()
        take_halo(1, HALO + LEAVES)

    @pl.when(jnp.logical_not(has_high))
    def _():
        no_halo(HALO + LEAVES)

    near_base = HALO - o * LEAVES

    def near_leaf(l):
        ids = [jnp.clip(nl[l, j] + near_base, 0, 2 * HALO + LEAVES - 1) for j in range(NEAR)]
        s = jnp.concatenate([srow[i] for i in ids], axis=0)[:, :ROWS]
        w = jnp.concatenate([swgt[i] for i in ids], axis=1)
        t = jnp.concatenate([gath[k, l] for k in range(BLKS)], axis=1)
        x = jnp.dot(s, t, preferred_element_type=F32)
        p = jnp.exp(x).astype(BF16)
        near_o[l] = jnp.dot(w, p, preferred_element_type=F32)

    def near_range(lo, hi):
        @pl.loop(lo, hi, unroll=2)
        def _(l):
            near_leaf(l)

    def skeleton_leaf(l):
        t = jnp.concatenate([gath[k, l] for k in range(BLKS)], axis=1)
        idx = si[pl.ds(l, 1), :]
        m = lax.broadcasted_iota(jnp.int32, (BLKS * PTS, SKEL), 0)
        hot = jnp.where(m == idx, 1.0, 0.0).astype(BF16)
        nat = jnp.dot(t, hot, preferred_element_type=F32)
        wgt = lax.dot_general(t[DIM:RAW], li[l], NT, preferred_element_type=F32)
        skel_o[l] = jnp.concatenate([nat[:DIM], wgt, nat[RAW:]], axis=0).astype(BF16)

    lane = lax.broadcasted_iota(jnp.int32, (ROWS, 128), 1)

    def quarter(l):
        v = skel_o[l].astype(F32)
        return jnp.where(parity == 0, v[:, :128], v[:, 128:])

    def far_pair(q):
        a = quarter(2 * q)
        c = quarter(2 * q + 1)
        a = jnp.where(half == 0, a, pltpu.roll(a, 64, axis=1))
        c = jnp.where(half == 1, c, pltpu.roll(c, 64, axis=1))
        fout[q] = jnp.where(lane < 64, a, c).astype(BF16)

    def far_copy(c, k):
        part = pl.ds(c * 2, 2)
        return remote(fout.at[part], fin.at[3 - k, part], far_send.at[c, k], far_recv.at[c, 3 - k],
                      o + STEPS[k], b)

    def far_wait(c, k):
        part = pl.ds(c * 2, 2)
        return remote(fout.at[part], fin.at[k, part], far_send.at[c, k], far_recv.at[c, k],
                      o + STEPS[k], b)

    li_copy.wait()
    opp = lax.rem(b + 2, BLKS)

    def chunk_work(c):
        @pl.loop(c * CHUNK, (c + 1) * CHUNK)
        def _(l):
            gath[up, l, RAW:ROWS, :] = aug_rows(gath[up, l, 0:DIM, :])
            gath[down, l, RAW:ROWS, :] = aug_rows(gath[down, l, 0:DIM, :])

        forward(c, 0).wait_recv()
        forward(c, 1).wait_recv()

        @pl.loop(c * CHUNK, (c + 1) * CHUNK, unroll=2)
        def _(l):
            gath[opp, l, RAW:ROWS, :] = aug_rows(gath[opp, l, 0:DIM, :])
            skeleton_leaf(l)

        @pl.loop(c * 2, c * 2 + 2)
        def _(q):
            far_pair(q)

        for k, step in enumerate(STEPS):
            @pl.when((o + step >= 0) & (o + step < OWNERS))
            def _():
                far_copy(c, k).start()

    for c in range(CHUNKS):
        direct[c][0].wait_recv()
        forward(c, 0).start()
        direct[c][1].wait_recv()
        forward(c, 1).start()
        if c + AHEAD < CHUNKS:
            direct[c + AHEAD][0].start()
            direct[c + AHEAD][1].start()
        if c > 0:
            chunk_work(c - 1)
            near_range((c - 1) * CHUNK, c * CHUNK)
    chunk_work(CHUNKS - 1)

    rt_copy.wait()
    ridx = ri[0:1, :]
    s_id = lax.broadcasted_iota(jnp.int32, (4 * SKEL, SKEL), 0)
    pts = jnp.zeros((ROWS, SKEL), F32)
    wgt = jnp.zeros((RHS, 128), F32)
    rows = pl.ds(pl.multiple_of(half * 128, 128), 128)
    for l in range(0, LEAVES, 4):
        hot = jnp.where(s_id == ridx - l * SKEL, 1.0, 0.0).astype(BF16)
        four = jnp.concatenate([skel_o[l + e] for e in range(4)], axis=1)
        lift = jnp.concatenate([rt[l + e, rows, :] for e in range(4)], axis=1)
        pts = pts + jnp.dot(four, hot, preferred_element_type=F32)
        wgt = wgt + lax.dot_general(four[DIM:RAW], lift, NT, preferred_element_type=F32)
    mine = jnp.where(half == 0, pts[:, :128], pts[:, 128:])

    @pl.when(sender)
    def _():
        rbuf[cx, cz] = jnp.concatenate([mine[:DIM], wgt, mine[RAW:]], axis=0).astype(BF16)

    def root_z(d):
        to = leaf_id(lax.rem(cz + d, 8), cx, core)
        ref = rbuf.at[cx, cz]
        return remote(ref, ref, z_send.at[d - 1], z_recv.at[d - 1], to, b)

    def root_z_wait(d):
        src = lax.rem(cz + 8 - d, 8)
        ref = rbuf.at[cx, src]
        return remote(ref, ref, z_send.at[d - 1], z_recv.at[d - 1], leaf_id(src, cx, core), b)

    def root_x(d):
        to = leaf_id(cz, lax.rem(cx + d, 4), core)
        ref = rbuf.at[cx]
        return remote(ref, ref, x_send.at[d - 1], x_recv.at[d - 1], to, b)

    def root_x_wait(d):
        src = lax.rem(cx + 4 - d, 4)
        ref = rbuf.at[src]
        return remote(ref, ref, x_send.at[d - 1], x_recv.at[d - 1], leaf_id(cz, src, core), b)

    def root_c(d):
        ref = rbuf.at[lax.rem(cx + 4 - d, 4)]
        return remote(ref, ref, c_send.at[d], c_recv.at[d], leaf_id(cz, cx, 1 - core), b)

    @pl.when(sender)
    def _():
        for d in range(1, 8):
            root_z(d).start()

    for h in range(2):
        v = pts[:, h * 128:(h + 1) * 128]
        rts[h * 128:(h + 1) * 128, :] = to_rows(v[:DIM], v[RAW:])

    near_range(12, 16)

    wlane = lax.broadcasted_iota(jnp.int32, (RHS, 128), 1)
    for k, step in enumerate(STEPS):
        exists = (o + step >= 0) & (o + step < OWNERS)

        @pl.when(exists)
        def _():
            for c in range(CHUNKS):
                far_wait(c, k).wait_recv()

            @pl.loop(0, 8)
            def _(q):
                v = fin[k, q]
                even = k * 16 + 2 * q
                rows = to_rows(v[:DIM], v[RAW:])
                fs[even] = rows[:64]
                fs[even + 1] = rows[64:]
                w = v[DIM:RAW].astype(F32)
                left = jnp.where(wlane < 64, w, 0.0)
                right = jnp.where(wlane < 64, 0.0, w)
                wl[even] = left
                wr[even] = pltpu.roll(left, 64, axis=1)
                wl[even + 1] = pltpu.roll(right, 64, axis=1)
                wr[even + 1] = right

        @pl.when(jnp.logical_not(exists))
        def _():
            @pl.loop(k * 16, k * 16 + 16)
            def _(e):
                fs[e] = jnp.zeros((64, 128), BF16)
                wl[e] = jnp.zeros((RHS, 128), F32)
                wr[e] = jnp.zeros((RHS, 128), F32)

    lists = fl_v[...]

    def named(u):
        f = fl_s[0, u]
        owner = f // LEAVES
        step = owner - o
        at = (step + 2 - jnp.where(step > 0, 1, 0)) * LEAVES + f - owner * LEAVES
        hit = jnp.max(jnp.where(lists == f, 1.0, 0.0), axis=1, keepdims=True)
        return jnp.clip(at, 0, 63), hit * jnp.where(step == 0, 0.0, 1.0)

    for v in range(PAIRS):
        at0, hit0 = named(2 * v)
        at1, hit1 = named(2 * v + 1)
        sall[v * 128:v * 128 + 64, :] = fs[at0]
        sall[v * 128 + 64:v * 128 + 128, :] = fs[at1]
        wall[:, v * 128:(v + 1) * 128] = wl[at0] + wr[at1]
        mask[:, v * 128:(v + 1) * 128] = jnp.where(wlane < 64, hit0, hit1)

    def far_range(lo, hi):
        @pl.loop(lo, hi, step=2)
        def _(l):
            t = jnp.concatenate([skel_o[l], skel_o[l + 1]], axis=1)
            w0 = (wall[...] * mask[pl.ds(l, 1), :]).astype(BF16)
            w1 = (wall[...] * mask[pl.ds(l + 1, 1), :]).astype(BF16)
            x = jnp.dot(sall[:, :ROWS], t, preferred_element_type=F32)
            p = jnp.exp(x).astype(BF16)
            farsum[l] = jnp.dot(w0, p[:, :SKEL], preferred_element_type=F32)
            farsum[l + 1] = jnp.dot(w1, p[:, SKEL:], preferred_element_type=F32)

    @pl.when(sender)
    def _():
        for d in range(1, 8):
            root_z_wait(d).wait_recv()
        for d in range(1, 4):
            root_x(d).start()
        root_c(0).start()

    far_range(0, 10)

    @pl.when(sender)
    def _():
        for d in range(1, 4):
            root_x_wait(d).wait_recv()
            root_c(d).start()

    far_range(10, 16)

    def scatter_copy(c, d):
        to = lax.rem(b + d, BLKS)
        return remote(part.at[to, leaves(c)], land.at[d - 1, leaves(c)],
                      s_send.at[c, d - 1], s_recv.at[c, d - 1], o, to)

    for c in range(CHUNKS):
        for l in range(c * CHUNK, (c + 1) * CHUNK):
            total = near_o[l] + jnp.dot(farsum[l].astype(BF16), li[l], preferred_element_type=F32)
            total = total.astype(BF16)
            for d in range(BLKS):
                part[d, l] = total[:, d * 128:(d + 1) * 128]
        for d in (2, 1, 3):
            scatter_copy(c, d).start()

    @pl.when(jnp.logical_not(sender))
    def _():
        for d in range(4):
            root_c(d).wait_recv()

    targets = rts[:, :ROWS]

    def root_group(i, acc):
        cols = []
        wgts = []
        for e in range(4):
            x = i // 2
            z = (i - 2 * x) * 4 + e
            p = leaf_id(z, x, parity)
            v = rbuf[x, z]
            cols.append(v)
            wgts.append(jnp.where(jnp.abs(p - o) > 2, v[DIM:RAW].astype(F32), 0.0).astype(BF16))
        xt = jnp.dot(targets, jnp.concatenate(cols, axis=1), preferred_element_type=F32)
        pt = jnp.exp(xt).astype(BF16)
        w = jnp.concatenate(wgts, axis=1)
        return acc + lax.dot_general(w, pt, NT, preferred_element_type=F32)

    rf = lax.fori_loop(0, 8, root_group, jnp.zeros((RHS, SKEL), F32), unroll=2).astype(BF16)

    rfs[b] = rf

    def root_sum(d):
        return remote(rfs.at[b], rfs.at[b], r_send.at[d - 1], r_recv.at[d - 1], o, lax.rem(b + d, BLKS))

    for d in range(1, BLKS):
        root_sum(d).start()
    for d in range(1, BLKS):
        root_sum(d).wait_recv()
    field = rfs[0].astype(F32)
    for d in range(1, BLKS):
        field = field + rfs[d].astype(F32)
    field = field.astype(BF16)
    mine = pl.ds(pl.multiple_of(b * 128, 128), 128)
    for c in range(CHUNKS):
        group = range(c * CHUNK, (c + 1) * CHUNK)
        lifted = [jnp.dot(field, rt[l], preferred_element_type=F32).astype(BF16) for l in group]
        for d in range(1, BLKS):
            scatter_copy(c, d).wait_recv()
        for l, v in zip(group, lifted):
            total = jnp.dot(v, li[l, :, mine], preferred_element_type=F32)
            total = total + part[b, l].astype(F32)
            for d in range(BLKS - 1):
                total = total + land[d, l].astype(F32)
            out[l] = total

    @pl.when(has_high)
    def _():
        h_up.wait_send()

    @pl.when(has_low)
    def _():
        h_down.wait_send()

    for c in range(CHUNKS):
        for k, step in enumerate(STEPS):
            @pl.when((o + step >= 0) & (o + step < OWNERS))
            def _():
                far_copy(c, k).wait_send()
        for d in (1, 2, 3):
            scatter_copy(c, d).wait_send()
        for k in range(2):
            direct[c][k].wait_send()
            forward(c, k).wait_send()

    for d in range(1, BLKS):
        root_sum(d).wait_send()

    @pl.when(sender)
    def _():
        for d in range(1, 8):
            root_z(d).wait_send()
        for d in range(1, 4):
            root_x(d).wait_send()
        for d in range(4):
            root_c(d).wait_send()


def on_device(points, charges, leaf_interp, root_interp, skeleton_index, root_index, near_list, far_list, far_count):
    vmem = pl.BlockSpec(memory_space=pltpu.VMEM)
    smem = pl.BlockSpec(memory_space=pltpu.SMEM)
    hbm = pl.BlockSpec(memory_space=pl.ANY)
    dma = pltpu.SemaphoreType.DMA

    out = pl.pallas_call(
        potential_kernel,
        out_shape=jax.ShapeDtypeStruct((LEAVES, RHS, PTS), F32),
        in_specs=[vmem, vmem, smem, smem, vmem, vmem, vmem, hbm, hbm],
        out_specs=vmem,
        scratch_shapes=[
            pltpu.VMEM((LEAVES, RAW, PTS), BF16),
            pltpu.VMEM((BLKS, LEAVES, ROWS, PTS), BF16),
            pltpu.VMEM((2, HALO, RAW, PTS), BF16),
            pltpu.VMEM((2 * HALO + LEAVES, 128, 128), BF16),
            pltpu.VMEM((2 * HALO + LEAVES, RHS, 128), BF16),
            pltpu.VMEM((LEAVES, SKEL, BLKS * PTS), BF16),
            pltpu.VMEM((LEAVES, SKEL, SKEL), BF16),
            pltpu.VMEM((8, ROWS, 128), BF16),
            pltpu.VMEM((4, 8, ROWS, 128), BF16),
            pltpu.VMEM((4, 8, ROWS, 128), BF16),
            pltpu.VMEM((LEAVES, RHS, BLKS * PTS), F32),
            pltpu.VMEM((LEAVES, ROWS, SKEL), BF16),
            pltpu.VMEM((64, 64, 128), BF16),
            pltpu.VMEM((64, RHS, 128), F32),
            pltpu.VMEM((64, RHS, 128), F32),
            pltpu.VMEM((SKEL, 128), BF16),
            pltpu.VMEM((PAIRS * 128, 128), BF16),
            pltpu.VMEM((RHS, PAIRS * 128), F32),
            pltpu.VMEM((LEAVES, PAIRS * 128), F32),
            pltpu.VMEM((LEAVES, RHS, SKEL), F32),
            pltpu.VMEM((BLKS, LEAVES, RHS, PTS), BF16),
            pltpu.VMEM((BLKS - 1, LEAVES, RHS, PTS), BF16),
            pltpu.VMEM((BLKS, RHS, SKEL), BF16),
            dma, dma,
            dma((CHUNKS, 2)), dma((CHUNKS, 2)), dma((CHUNKS, 2)), dma((CHUNKS, 2)),
            dma((2,)), dma((2,)),
            dma((CHUNKS, 4)), dma((CHUNKS, 4)),
            dma((7,)), dma((7,)), dma((3,)), dma((3,)), dma((4,)), dma((4,)),
            dma((CHUNKS, 3)), dma((CHUNKS, 3)), dma((3,)), dma((3,)),
        ],
        compiler_params=pltpu.CompilerParams(
            collective_id=0, has_side_effects=True, vmem_limit_bytes=VMEM_LIMIT),
    )(points, charges, near_list, far_list, far_list, skeleton_index, root_index, leaf_interp, root_interp)
    return jnp.transpose(out, (1, 0, 2))


def solution(mesh):
    placed = (
        P(None, "leaf", "blk"),
        P(None, "leaf", "blk"),
        P("leaf", None, None),
        P("leaf", None, None),
        P("leaf", None),
        P("leaf", None),
        P("leaf", None),
        P("leaf", None),
        P("leaf"),
    )
    return jax.shard_map(
        on_device, mesh=mesh, in_specs=placed, out_specs=P(None, "leaf", "blk"), check_vma=False
    )
```

```python
import jax
import jax.numpy as jnp
from jax import lax
from jax.experimental import pallas as pl
from jax.experimental.pallas import tpu as pltpu
from jax.sharding import PartitionSpec as P

MESH = pl.DeviceIdType.MESH
F32 = jnp.float32
BF16 = jnp.bfloat16
NT = (((1,), (1,)), ((), ()))

DIM = 64
RHS = 16
RAW = DIM + RHS
ROWS = 96
LEAVES = 16
PTS = 128
BLKS = 4
SKEL = 256
HALO = 8
NEAR = 10
FAR = 32
OWNERS = 64
CHUNKS = 8
CHUNK = LEAVES // CHUNKS
QUADS = 4
QUAD = LEAVES // QUADS
STEPS = (-2, -1, 1, 2)
PAIRS = FAR // 2
FAR_A = 10
FAR_B = 12
VMEM_LIMIT = 58 * 2**20


def aug_rows(points):
    p = points.astype(F32)
    n = -0.5 * jnp.sum(p * p, axis=0, keepdims=True)
    hi = n.astype(BF16).astype(F32)
    rest = n - hi
    mid = rest.astype(BF16).astype(F32)
    low = rest - mid
    row = lax.broadcasted_iota(jnp.int32, (16, n.shape[1]), 0)
    out = jnp.where(row == 0, hi, jnp.where(row == 1, mid, jnp.where(row == 2, low, 0.0)))
    out = jnp.where((row >= 4) & (row < 7), 1.0, out)
    return out.astype(BF16)


def to_rows(points, aug):
    a = aug.astype(F32)[:8]
    swapped = jnp.concatenate([a[4:], a[:4]], axis=0)
    z16 = jnp.zeros((16, 128), F32)
    z40 = jnp.zeros((40, 128), F32)
    full = jnp.concatenate([points.astype(F32), z16, swapped, z40], axis=0)
    return full.T.astype(BF16)


def leaf_id(z, x, c):
    return (z * 4 + x) * 2 + c


def potential_kernel(
    points_hbm, charges_hbm, nl, fl_s, fl_v, si, ri, li_hbm, rt_hbm,
    out,
    points, charges, own, gath, halo, srow, swgt, li, rt, fout, fin, rbuf,
    near_o, skel_o, fs, wl, wr, rts, sall, wall, mask, farsum, part, land, rfs,
    p_sem, q_sem, li_sem, rt_sem, y_send, y_recv, h_send, h_recv,
    far_send, far_recv, z_send, z_recv, x_send, x_recv, c_send, c_recv, s_send, s_recv, r_send, r_recv,
):
    o = lax.axis_index("leaf")
    b = lax.axis_index("blk")
    core = lax.rem(o, 2)
    cx = lax.rem(o // 2, 4)
    cz = o // 8
    up = lax.rem(b + 1, BLKS)
    down = lax.rem(b + BLKS - 1, BLKS)
    half = lax.rem(b, 2)
    parity = b // 2
    sender = core == parity

    li_copy = pltpu.make_async_copy(li_hbm, li, li_sem)
    rt_copy = pltpu.make_async_copy(rt_hbm, rt, rt_sem)
    p_copy = pltpu.make_async_copy(points_hbm, points, p_sem)
    q_copy = pltpu.make_async_copy(charges_hbm, charges, q_sem)
    p_copy.start()
    q_copy.start()

    barrier = pltpu.get_barrier_semaphore()

    def greet(leaf, blk):
        pl.semaphore_signal(barrier, inc=1, device_id=(leaf, blk), device_id_type=MESH)

    greet(o, up)
    greet(o, down)
    for d in range(1, 8):
        greet(leaf_id(lax.rem(cz + d, 8), cx, core), b)
    for d in range(1, 4):
        greet(leaf_id(cz, lax.rem(cx + d, 4), core), b)
    greet(leaf_id(cz, cx, 1 - core), b)
    greet(o, lax.rem(b + 2, BLKS))
    for step in STEPS:
        @pl.when((o + step >= 0) & (o + step < OWNERS))
        def _():
            greet(o + step, b)

    p_copy.wait()
    q_copy.wait()
    li_copy.start()
    rt_copy.start()
    for h in range(2):
        for g in range(DIM // 16):
            v = points[g * 16:(g + 1) * 16, h * 8:(h + 1) * 8, :].astype(F32)
            own[h * 8:(h + 1) * 8, g * 16:(g + 1) * 16, :] = jnp.swapaxes(v, 0, 1).astype(BF16)
        v = charges[:, h * 8:(h + 1) * 8, :].astype(F32)
        own[h * 8:(h + 1) * 8, DIM:RAW, :] = jnp.swapaxes(v, 0, 1).astype(BF16)

    @pl.loop(0, LEAVES, unroll=2)
    def _(l):
        raw = own[l]
        aug = aug_rows(raw[:DIM])
        gath[b, l, 0:RAW, :] = raw
        gath[b, l, RAW:ROWS, :] = aug
        srow[HALO + l] = to_rows(raw[:DIM], aug)
        swgt[HALO + l] = raw[DIM:]

    pl.semaphore_wait(barrier, 14 + jnp.minimum(o, 2) + jnp.minimum(OWNERS - 1 - o, 2))

    def remote(src, dst, ssem, rsem, leaf, blk):
        return pltpu.make_async_remote_copy(
            src_ref=src, dst_ref=dst, send_sem=ssem, recv_sem=rsem,
            device_id=(leaf, blk), device_id_type=MESH)

    has_low = o > 0
    has_high = o < OWNERS - 1
    h_up = remote(own.at[pl.ds(LEAVES - HALO, HALO)], halo.at[0], h_send.at[0], h_recv.at[0], o + 1, b)
    h_down = remote(own.at[pl.ds(0, HALO)], halo.at[1], h_send.at[1], h_recv.at[1], o - 1, b)

    @pl.when(has_high)
    def _():
        h_up.start()

    @pl.when(has_low)
    def _():
        h_down.start()

    def leaves(c):
        return pl.ds(c * CHUNK, CHUNK)

    def gather_copy(c, d):
        return remote(own.at[leaves(c)], gath.at[b, leaves(c), pl.ds(0, RAW)],
                      y_send.at[c, d - 1], y_recv.at[c, d - 1], o, lax.rem(b + d, BLKS))

    def leaves(c):
        return pl.ds(c * CHUNK, CHUNK)

    for c in range(CHUNKS):
        for d in (2, 1, 3):
            gather_copy(c, d).start()

    def take_halo(side, at):
        @pl.loop(0, HALO)
        def _(l):
            raw = halo[side, l]
            srow[at + l] = to_rows(raw[:DIM], aug_rows(raw[:DIM]))
            swgt[at + l] = raw[DIM:]

    def no_halo(at):
        @pl.loop(0, HALO)
        def _(l):
            srow[at + l] = jnp.zeros((128, 128), BF16)
            swgt[at + l] = jnp.zeros((RHS, 128), BF16)

    near_base = HALO - o * LEAVES

    def near_leaf(l):
        ids = [jnp.clip(nl[l, j] + near_base, 0, 2 * HALO + LEAVES - 1) for j in range(NEAR)]
        s = jnp.concatenate([srow[i] for i in ids], axis=0)[:, :ROWS]
        w = jnp.concatenate([swgt[i] for i in ids], axis=1)
        t = jnp.concatenate([gath[k, l] for k in range(BLKS)], axis=1)
        x = jnp.dot(s, t, preferred_element_type=F32)
        p = jnp.exp(x).astype(BF16)
        near_o[l] = jnp.dot(w, p, preferred_element_type=F32)

    def near_chunk(c):
        @pl.loop(0, CHUNK, unroll=2)
        def _(i):
            near_leaf(c * CHUNK + i)

    def skeleton_leaf(l):
        t = jnp.concatenate([gath[k, l] for k in range(BLKS)], axis=1)
        idx = si[pl.ds(l, 1), :]
        m = lax.broadcasted_iota(jnp.int32, (BLKS * PTS, SKEL), 0)
        hot = jnp.where(m == idx, 1.0, 0.0).astype(BF16)
        nat = jnp.dot(t, hot, preferred_element_type=F32)
        wgt = lax.dot_general(t[DIM:RAW], li[l], NT, preferred_element_type=F32)
        skel_o[l] = jnp.concatenate([nat[:DIM], wgt, nat[RAW:]], axis=0).astype(BF16)

    lane = lax.broadcasted_iota(jnp.int32, (ROWS, 128), 1)

    def quarter(l):
        v = skel_o[l].astype(F32)
        return jnp.where(parity == 0, v[:, :128], v[:, 128:])

    def far_pair(q):
        a = quarter(2 * q)
        c = quarter(2 * q + 1)
        a = jnp.where(half == 0, a, pltpu.roll(a, 64, axis=1))
        c = jnp.where(half == 1, c, pltpu.roll(c, 64, axis=1))
        fout[q] = jnp.where(lane < 64, a, c).astype(BF16)

    def far_copy(c, k):
        part = pl.ds(c * (CHUNK // 2), CHUNK // 2)
        return remote(fout.at[part], fin.at[3 - k, part], far_send.at[c, k], far_recv.at[c, 3 - k],
                      o + STEPS[k], b)

    def far_wait(c, k):
        part = pl.ds(c * (CHUNK // 2), CHUNK // 2)
        return remote(fout.at[part], fin.at[k, part], far_send.at[c, k], far_recv.at[c, k],
                      o + STEPS[k], b)

    opp = lax.rem(b + 2, BLKS)

    def chunk_work(c):
        for d in (2, 1, 3):
            gather_copy(c, d).wait_recv()

        @pl.loop(0, CHUNK, unroll=2)
        def _(i):
            l = c * CHUNK + i
            gath[up, l, RAW:ROWS, :] = aug_rows(gath[up, l, 0:DIM, :])
            gath[down, l, RAW:ROWS, :] = aug_rows(gath[down, l, 0:DIM, :])
            gath[opp, l, RAW:ROWS, :] = aug_rows(gath[opp, l, 0:DIM, :])
            skeleton_leaf(l)

        @pl.loop(0, CHUNK // 2)
        def _(i):
            far_pair(c * (CHUNK // 2) + i)

        for k, step in enumerate(STEPS):
            @pl.when((o + step >= 0) & (o + step < OWNERS))
            def _():
                far_copy(c, k).start()

    def halo_rows():
        @pl.when(has_low)
        def _():
            h_up.wait_recv()
            take_halo(0, 0)

        @pl.when(jnp.logical_not(has_low))
        def _():
            no_halo(0)

        @pl.when(has_high)
        def _():
            h_down.wait_recv()
            take_halo(1, HALO + LEAVES)

        @pl.when(jnp.logical_not(has_high))
        def _():
            no_halo(HALO + LEAVES)

    halo_rows()
    li_copy.wait()

    @pl.loop(0, CHUNKS - 1)
    def _(c):
        chunk_work(c)
        near_chunk(c)

    chunk_work(CHUNKS - 1)

    rt_copy.wait()
    ridx = ri[0:1, :]
    s_id = lax.broadcasted_iota(jnp.int32, (4 * SKEL, SKEL), 0)
    pts = jnp.zeros((ROWS, SKEL), F32)
    wgt = jnp.zeros((RHS, 128), F32)
    rows = pl.ds(pl.multiple_of(half * 128, 128), 128)
    for l in range(0, LEAVES, 4):
        hot = jnp.where(s_id == ridx - l * SKEL, 1.0, 0.0).astype(BF16)
        four = jnp.concatenate([skel_o[l + e] for e in range(4)], axis=1)
        lift = jnp.concatenate([rt[l + e, rows, :] for e in range(4)], axis=1)
        pts = pts + jnp.dot(four, hot, preferred_element_type=F32)
        wgt = wgt + lax.dot_general(four[DIM:RAW], lift, NT, preferred_element_type=F32)
    mine = jnp.where(half == 0, pts[:, :128], pts[:, 128:])

    @pl.when(sender)
    def _():
        rbuf[cx, cz] = jnp.concatenate([mine[:DIM], wgt, mine[RAW:]], axis=0).astype(BF16)

    def root_z(d):
        to = leaf_id(lax.rem(cz + d, 8), cx, core)
        ref = rbuf.at[cx, cz]
        return remote(ref, ref, z_send.at[d - 1], z_recv.at[d - 1], to, b)

    def root_z_wait(d):
        src = lax.rem(cz + 8 - d, 8)
        ref = rbuf.at[cx, src]
        return remote(ref, ref, z_send.at[d - 1], z_recv.at[d - 1], leaf_id(src, cx, core), b)

    def root_x(d):
        to = leaf_id(cz, lax.rem(cx + d, 4), core)
        ref = rbuf.at[cx]
        return remote(ref, ref, x_send.at[d - 1], x_recv.at[d - 1], to, b)

    def root_x_wait(d):
        src = lax.rem(cx + 4 - d, 4)
        ref = rbuf.at[src]
        return remote(ref, ref, x_send.at[d - 1], x_recv.at[d - 1], leaf_id(cz, src, core), b)

    def root_c(d):
        ref = rbuf.at[lax.rem(cx + 4 - d, 4)]
        return remote(ref, ref, c_send.at[d], c_recv.at[d], leaf_id(cz, cx, 1 - core), b)

    @pl.when(sender)
    def _():
        for d in range(1, 8):
            root_z(d).start()

    for h in range(2):
        v = pts[:, h * 128:(h + 1) * 128]
        rts[h * 128:(h + 1) * 128, :] = to_rows(v[:DIM], v[RAW:])

    near_chunk(CHUNKS - 1)

    wlane = lax.broadcasted_iota(jnp.int32, (RHS, 128), 1)
    for k, step in enumerate(STEPS):
        exists = (o + step >= 0) & (o + step < OWNERS)

        @pl.when(exists)
        def _():
            for c in range(CHUNKS):
                far_wait(c, k).wait_recv()

            @pl.loop(0, 8)
            def _(q):
                v = fin[k, q]
                even = k * 16 + 2 * q
                rows = to_rows(v[:DIM], v[RAW:])
                fs[even] = rows[:64]
                fs[even + 1] = rows[64:]
                w = v[DIM:RAW].astype(F32)
                left = jnp.where(wlane < 64, w, 0.0)
                right = jnp.where(wlane < 64, 0.0, w)
                wl[even] = left
                wr[even] = pltpu.roll(left, 64, axis=1)
                wl[even + 1] = pltpu.roll(right, 64, axis=1)
                wr[even + 1] = right

        @pl.when(jnp.logical_not(exists))
        def _():
            @pl.loop(k * 16, k * 16 + 16)
            def _(e):
                fs[e] = jnp.zeros((64, 128), BF16)
                wl[e] = jnp.zeros((RHS, 128), F32)
                wr[e] = jnp.zeros((RHS, 128), F32)

    lists = fl_v[...]

    def named(u):
        f = fl_s[0, u]
        owner = f // LEAVES
        step = owner - o
        at = (step + 2 - jnp.where(step > 0, 1, 0)) * LEAVES + f - owner * LEAVES
        hit = jnp.max(jnp.where(lists == f, 1.0, 0.0), axis=1, keepdims=True)
        return jnp.clip(at, 0, 63), hit * jnp.where(step == 0, 0.0, 1.0)

    for v in range(PAIRS):
        at0, hit0 = named(2 * v)
        at1, hit1 = named(2 * v + 1)
        sall[v * 128:v * 128 + 64, :] = fs[at0]
        sall[v * 128 + 64:v * 128 + 128, :] = fs[at1]
        wall[:, v * 128:(v + 1) * 128] = wl[at0] + wr[at1]
        mask[:, v * 128:(v + 1) * 128] = jnp.where(wlane < 64, hit0, hit1)

    def far_range(lo, hi):
        @pl.loop(lo, hi, step=2)
        def _(l):
            t = jnp.concatenate([skel_o[l], skel_o[l + 1]], axis=1)
            w0 = (wall[...] * mask[pl.ds(l, 1), :]).astype(BF16)
            w1 = (wall[...] * mask[pl.ds(l + 1, 1), :]).astype(BF16)
            x = jnp.dot(sall[:, :ROWS], t, preferred_element_type=F32)
            p = jnp.exp(x).astype(BF16)
            farsum[l] = jnp.dot(w0, p[:, :SKEL], preferred_element_type=F32)
            farsum[l + 1] = jnp.dot(w1, p[:, SKEL:], preferred_element_type=F32)

    @pl.when(sender)
    def _():
        for d in range(1, 8):
            root_z_wait(d).wait_recv()
        for d in range(1, 4):
            root_x(d).start()
        root_c(0).start()

    def scatter_copy(c, d):
        to = lax.rem(b + d, BLKS)
        return remote(part.at[to, pl.ds(c * QUAD, QUAD)], land.at[d - 1, pl.ds(c * QUAD, QUAD)],
                      s_send.at[c, d - 1], s_recv.at[c, d - 1], o, to)

    def far_down(c):
        for l in range(c * QUAD, (c + 1) * QUAD):
            total = near_o[l] + jnp.dot(farsum[l].astype(BF16), li[l], preferred_element_type=F32)
            total = total.astype(BF16)
            for d in range(BLKS):
                part[d, l] = total[:, d * 128:(d + 1) * 128]
        for d in (2, 1, 3):
            scatter_copy(c, d).start()

    far_range(0, FAR_A)
    @pl.when(sender)
    def _():
        for d in range(1, 4):
            root_x_wait(d).wait_recv()
            root_c(d).start()

    far_range(FAR_A, FAR_B)
    for c in range(FAR_B // QUAD):
        far_down(c)

    @pl.when(jnp.logical_not(sender))
    def _():
        for d in range(4):
            root_c(d).wait_recv()

    targets = rts[:, :ROWS]

    def root_group(i, acc):
        cols = []
        wgts = []
        for e in range(4):
            x = i // 2
            z = (i - 2 * x) * 4 + e
            p = leaf_id(z, x, parity)
            v = rbuf[x, z]
            cols.append(v)
            wgts.append(jnp.where(jnp.abs(p - o) > 2, v[DIM:RAW].astype(F32), 0.0).astype(BF16))
        xt = jnp.dot(targets, jnp.concatenate(cols, axis=1), preferred_element_type=F32)
        pt = jnp.exp(xt).astype(BF16)
        w = jnp.concatenate(wgts, axis=1)
        return acc + lax.dot_general(w, pt, NT, preferred_element_type=F32)

    rf = lax.fori_loop(0, 8, root_group, jnp.zeros((RHS, SKEL), F32), unroll=2).astype(BF16)

    rfs[b] = rf

    def root_sum(d):
        return remote(rfs.at[b], rfs.at[b], r_send.at[d - 1], r_recv.at[d - 1], o, lax.rem(b + d, BLKS))

    for d in range(1, BLKS):
        root_sum(d).start()
    far_range(FAR_B, LEAVES)
    for c in range(FAR_B // QUAD, QUADS):
        far_down(c)

    for d in range(1, BLKS):
        root_sum(d).wait_recv()
    field = rfs[0].astype(F32)
    for d in range(1, BLKS):
        field = field + rfs[d].astype(F32)
    field = field.astype(BF16)
    mine = pl.ds(pl.multiple_of(b * 128, 128), 128)
    for c in range(QUADS):
        group = range(c * QUAD, (c + 1) * QUAD)
        lifted = [jnp.dot(field, rt[l], preferred_element_type=F32).astype(BF16) for l in group]
        for d in range(1, BLKS):
            scatter_copy(c, d).wait_recv()
        for l, v in zip(group, lifted):
            total = jnp.dot(v, li[l, :, mine], preferred_element_type=F32)
            total = total + part[b, l].astype(F32)
            for d in range(BLKS - 1):
                total = total + land[d, l].astype(F32)
            out[l] = total

    @pl.when(has_high)
    def _():
        h_up.wait_send()

    @pl.when(has_low)
    def _():
        h_down.wait_send()

    for c in range(CHUNKS):
        for k, step in enumerate(STEPS):
            @pl.when((o + step >= 0) & (o + step < OWNERS))
            def _():
                far_copy(c, k).wait_send()
        for d in (1, 2, 3):
            gather_copy(c, d).wait_send()

    for d in range(1, BLKS):
        root_sum(d).wait_send()
        for c in range(QUADS):
            scatter_copy(c, d).wait_send()

    @pl.when(sender)
    def _():
        for d in range(1, 8):
            root_z(d).wait_send()
        for d in range(1, 4):
            root_x(d).wait_send()
        for d in range(4):
            root_c(d).wait_send()


def on_device(points, charges, leaf_interp, root_interp, skeleton_index, root_index, near_list, far_list, far_count):
    vmem = pl.BlockSpec(memory_space=pltpu.VMEM)
    smem = pl.BlockSpec(memory_space=pltpu.SMEM)
    hbm = pl.BlockSpec(memory_space=pl.ANY)
    dma = pltpu.SemaphoreType.DMA

    out = pl.pallas_call(
        potential_kernel,
        out_shape=jax.ShapeDtypeStruct((LEAVES, RHS, PTS), F32),
        in_specs=[hbm, hbm, smem, smem, vmem, vmem, vmem, hbm, hbm],
        out_specs=vmem,
        scratch_shapes=[
            pltpu.VMEM((DIM, LEAVES, PTS), BF16),
            pltpu.VMEM((RHS, LEAVES, PTS), BF16),
            pltpu.VMEM((LEAVES, RAW, PTS), BF16),
            pltpu.VMEM((BLKS, LEAVES, ROWS, PTS), BF16),
            pltpu.VMEM((2, HALO, RAW, PTS), BF16),
            pltpu.VMEM((2 * HALO + LEAVES, 128, 128), BF16),
            pltpu.VMEM((2 * HALO + LEAVES, RHS, 128), BF16),
            pltpu.VMEM((LEAVES, SKEL, BLKS * PTS), BF16),
            pltpu.VMEM((LEAVES, SKEL, SKEL), BF16),
            pltpu.VMEM((8, ROWS, 128), BF16),
            pltpu.VMEM((4, 8, ROWS, 128), BF16),
            pltpu.VMEM((4, 8, ROWS, 128), BF16),
            pltpu.VMEM((LEAVES, RHS, BLKS * PTS), F32),
            pltpu.VMEM((LEAVES, ROWS, SKEL), BF16),
            pltpu.VMEM((64, 64, 128), BF16),
            pltpu.VMEM((64, RHS, 128), F32),
            pltpu.VMEM((64, RHS, 128), F32),
            pltpu.VMEM((SKEL, 128), BF16),
            pltpu.VMEM((PAIRS * 128, 128), BF16),
            pltpu.VMEM((RHS, PAIRS * 128), F32),
            pltpu.VMEM((LEAVES, PAIRS * 128), F32),
            pltpu.VMEM((LEAVES, RHS, SKEL), F32),
            pltpu.VMEM((BLKS, LEAVES, RHS, PTS), BF16),
            pltpu.VMEM((BLKS - 1, LEAVES, RHS, PTS), BF16),
            pltpu.VMEM((BLKS, RHS, SKEL), BF16),
            dma, dma, dma, dma,
            dma((CHUNKS, 3)), dma((CHUNKS, 3)),
            dma((2,)), dma((2,)),
            dma((CHUNKS, 4)), dma((CHUNKS, 4)),
            dma((7,)), dma((7,)), dma((3,)), dma((3,)), dma((4,)), dma((4,)),
            dma((QUADS, 3)), dma((QUADS, 3)), dma((3,)), dma((3,)),
        ],
        compiler_params=pltpu.CompilerParams(
            collective_id=0, has_side_effects=True, vmem_limit_bytes=VMEM_LIMIT),
    )(points, charges, near_list, far_list, far_list, skeleton_index, root_index, leaf_interp, root_interp)
    return jnp.transpose(out, (1, 0, 2))


def solution(mesh):
    placed = (
        P(None, "leaf", "blk"),
        P(None, "leaf", "blk"),
        P("leaf", None, None),
        P("leaf", None, None),
        P("leaf", None),
        P("leaf", None),
        P("leaf", None),
        P("leaf", None),
        P("leaf"),
    )
    return jax.shard_map(
        on_device, mesh=mesh, in_specs=placed, out_specs=P(None, "leaf", "blk"), check_vma=False
    )
```

```python
import jax
import jax.numpy as jnp
from jax import lax
from jax.experimental import pallas as pl
from jax.experimental.pallas import tpu as pltpu
from jax.sharding import PartitionSpec as P

MESH = pl.DeviceIdType.MESH
F32 = jnp.float32
BF16 = jnp.bfloat16
NT = (((1,), (1,)), ((), ()))

DIM = 64
RHS = 16
RAW = DIM + RHS
ROWS = 96
LEAVES = 16
PTS = 128
BLKS = 4
SKEL = 256
HALO = 8
NEAR = 10
FAR = 32
OWNERS = 64
CHUNKS = 8
CHUNK = LEAVES // CHUNKS
QUADS = 4
QUAD = LEAVES // QUADS
STEPS = (-2, -1, 1, 2)
PAIRS = FAR // 2
FAR_A = 10
FAR_B = 12
VMEM_LIMIT = 58 * 2**20


def aug_rows(points):
    p = points.astype(F32)
    n = -0.5 * jnp.sum(p * p, axis=0, keepdims=True)
    hi = n.astype(BF16).astype(F32)
    rest = n - hi
    mid = rest.astype(BF16).astype(F32)
    low = rest - mid
    row = lax.broadcasted_iota(jnp.int32, (16, n.shape[1]), 0)
    out = jnp.where(row == 0, hi, jnp.where(row == 1, mid, jnp.where(row == 2, low, 0.0)))
    out = jnp.where((row >= 4) & (row < 7), 1.0, out)
    return out.astype(BF16)


def to_rows(points, aug):
    a = aug.astype(F32)[:8]
    swapped = jnp.concatenate([a[4:], a[:4]], axis=0)
    z16 = jnp.zeros((16, 128), F32)
    z40 = jnp.zeros((40, 128), F32)
    full = jnp.concatenate([points.astype(F32), z16, swapped, z40], axis=0)
    return full.T.astype(BF16)


def leaf_id(z, x, c):
    return (z * 4 + x) * 2 + c


def potential_kernel(
    points_hbm, charges_hbm, nl, fl_s, fl_v, si, ri, li_hbm, rt_hbm,
    out,
    points, charges, own, gath, halo, srow, swgt, li, rt, fout, fin, rbuf,
    near_o, skel_o, fs, wl, wr, rts, sall, wall, mask, farsum, part, land, rfs,
    p_sem, q_sem, li_sem, rt_sem, y_send, y_recv, h_send, h_recv,
    far_send, far_recv, z_send, z_recv, x_send, x_recv, c_send, c_recv, s_send, s_recv, r_send, r_recv,
):
    o = lax.axis_index("leaf")
    b = lax.axis_index("blk")
    core = lax.rem(o, 2)
    cx = lax.rem(o // 2, 4)
    cz = o // 8
    up = lax.rem(b + 1, BLKS)
    down = lax.rem(b + BLKS - 1, BLKS)
    half = lax.rem(b, 2)
    parity = b // 2
    sender = core == parity

    li_copy = pltpu.make_async_copy(li_hbm, li, li_sem)
    rt_copy = pltpu.make_async_copy(rt_hbm, rt, rt_sem)
    p_copy = pltpu.make_async_copy(points_hbm, points, p_sem)
    q_copy = pltpu.make_async_copy(charges_hbm, charges, q_sem)
    p_copy.start()
    q_copy.start()

    barrier = pltpu.get_barrier_semaphore()

    def greet(leaf, blk):
        pl.semaphore_signal(barrier, inc=1, device_id=(leaf, blk), device_id_type=MESH)

    greet(o, up)
    greet(o, down)
    for d in range(1, 8):
        greet(leaf_id(lax.rem(cz + d, 8), cx, core), b)
    for d in range(1, 4):
        greet(leaf_id(cz, lax.rem(cx + d, 4), core), b)
    greet(leaf_id(cz, cx, 1 - core), b)
    greet(o, lax.rem(b + 2, BLKS))
    for step in STEPS:
        @pl.when((o + step >= 0) & (o + step < OWNERS))
        def _():
            greet(o + step, b)

    p_copy.wait()
    q_copy.wait()
    li_copy.start()
    rt_copy.start()
    for h in range(2):
        for g in range(DIM // 16):
            v = points[g * 16:(g + 1) * 16, h * 8:(h + 1) * 8, :].astype(F32)
            own[h * 8:(h + 1) * 8, g * 16:(g + 1) * 16, :] = jnp.swapaxes(v, 0, 1).astype(BF16)
        v = charges[:, h * 8:(h + 1) * 8, :].astype(F32)
        own[h * 8:(h + 1) * 8, DIM:RAW, :] = jnp.swapaxes(v, 0, 1).astype(BF16)

    pl.semaphore_wait(barrier, 14 + jnp.minimum(o, 2) + jnp.minimum(OWNERS - 1 - o, 2))

    def remote(src, dst, ssem, rsem, leaf, blk):
        return pltpu.make_async_remote_copy(
            src_ref=src, dst_ref=dst, send_sem=ssem, recv_sem=rsem,
            device_id=(leaf, blk), device_id_type=MESH)

    has_low = o > 0
    has_high = o < OWNERS - 1
    h_up = remote(own.at[pl.ds(LEAVES - HALO, HALO)], halo.at[0], h_send.at[0], h_recv.at[0], o + 1, b)
    h_down = remote(own.at[pl.ds(0, HALO)], halo.at[1], h_send.at[1], h_recv.at[1], o - 1, b)

    @pl.when(has_high)
    def _():
        h_up.start()

    @pl.when(has_low)
    def _():
        h_down.start()

    def leaves(c):
        return pl.ds(c * CHUNK, CHUNK)

    def gather_copy(c, d):
        return remote(own.at[leaves(c)], gath.at[b, leaves(c), pl.ds(0, RAW)],
                      y_send.at[c, d - 1], y_recv.at[c, d - 1], o, lax.rem(b + d, BLKS))

    def leaves(c):
        return pl.ds(c * CHUNK, CHUNK)

    for c in range(CHUNKS):
        for d in (2, 1, 3):
            gather_copy(c, d).start()

    def take_halo(side, at):
        @pl.loop(0, HALO, unroll=8)
        def _(l):
            raw = halo[side, l]
            srow[at + l] = to_rows(raw[:DIM], aug_rows(raw[:DIM]))
            swgt[at + l] = raw[DIM:]

    def no_halo(at):
        @pl.loop(0, HALO)
        def _(l):
            srow[at + l] = jnp.zeros((128, 128), BF16)
            swgt[at + l] = jnp.zeros((RHS, 128), BF16)

    near_base = HALO - o * LEAVES

    def near_leaf(l):
        ids = [jnp.clip(nl[l, j] + near_base, 0, 2 * HALO + LEAVES - 1) for j in range(NEAR)]
        s = jnp.concatenate([srow[i] for i in ids], axis=0)[:, :ROWS]
        w = jnp.concatenate([swgt[i] for i in ids], axis=1)
        t = jnp.concatenate([gath[k, l] for k in range(BLKS)], axis=1)
        x = jnp.dot(s, t, preferred_element_type=F32)
        p = jnp.exp(x).astype(BF16)
        near_o[l] = jnp.dot(w, p, preferred_element_type=F32)

    def near_chunk(c):
        @pl.loop(0, CHUNK, unroll=2)
        def _(i):
            near_leaf(c * CHUNK + i)

    def skeleton_leaf(l):
        t = jnp.concatenate([gath[k, l] for k in range(BLKS)], axis=1)
        idx = si[pl.ds(l, 1), :]
        m = lax.broadcasted_iota(jnp.int32, (BLKS * PTS, SKEL), 0)
        hot = jnp.where(m == idx, 1.0, 0.0).astype(BF16)
        nat = jnp.dot(t, hot, preferred_element_type=F32)
        wgt = lax.dot_general(t[DIM:RAW], li[l], NT, preferred_element_type=F32)
        skel_o[l] = jnp.concatenate([nat[:DIM], wgt, nat[RAW:]], axis=0).astype(BF16)

    lane = lax.broadcasted_iota(jnp.int32, (ROWS, 128), 1)

    def quarter(l):
        v = skel_o[l].astype(F32)
        return jnp.where(parity == 0, v[:, :128], v[:, 128:])

    def far_pair(q):
        a = quarter(2 * q)
        c = quarter(2 * q + 1)
        a = jnp.where(half == 0, a, pltpu.roll(a, 64, axis=1))
        c = jnp.where(half == 1, c, pltpu.roll(c, 64, axis=1))
        fout[q] = jnp.where(lane < 64, a, c).astype(BF16)

    def far_copy(c, k):
        part = pl.ds(c * (CHUNK // 2), CHUNK // 2)
        return remote(fout.at[part], fin.at[3 - k, part], far_send.at[c, k], far_recv.at[c, 3 - k],
                      o + STEPS[k], b)

    def far_wait(c, k):
        part = pl.ds(c * (CHUNK // 2), CHUNK // 2)
        return remote(fout.at[part], fin.at[k, part], far_send.at[c, k], far_recv.at[c, k],
                      o + STEPS[k], b)

    opp = lax.rem(b + 2, BLKS)

    def chunk_work(c):
        for d in (2, 1, 3):
            gather_copy(c, d).wait_recv()

        @pl.loop(0, CHUNK, unroll=2)
        def _(i):
            l = c * CHUNK + i
            gath[up, l, RAW:ROWS, :] = aug_rows(gath[up, l, 0:DIM, :])
            gath[down, l, RAW:ROWS, :] = aug_rows(gath[down, l, 0:DIM, :])
            gath[opp, l, RAW:ROWS, :] = aug_rows(gath[opp, l, 0:DIM, :])
            skeleton_leaf(l)

        @pl.loop(0, CHUNK // 2)
        def _(i):
            far_pair(c * (CHUNK // 2) + i)

        for k, step in enumerate(STEPS):
            @pl.when((o + step >= 0) & (o + step < OWNERS))
            def _():
                far_copy(c, k).start()

    def halo_rows():
        @pl.when(has_low)
        def _():
            h_up.wait_recv()
            take_halo(0, 0)

        @pl.when(jnp.logical_not(has_low))
        def _():
            no_halo(0)

        @pl.when(has_high)
        def _():
            h_down.wait_recv()
            take_halo(1, HALO + LEAVES)

        @pl.when(jnp.logical_not(has_high))
        def _():
            no_halo(HALO + LEAVES)

    @pl.loop(0, LEAVES, unroll=4)
    def _(l):
        raw = own[l]
        aug = aug_rows(raw[:DIM])
        gath[b, l, 0:RAW, :] = raw
        gath[b, l, RAW:ROWS, :] = aug
        srow[HALO + l] = to_rows(raw[:DIM], aug)
        swgt[HALO + l] = raw[DIM:]

    halo_rows()
    li_copy.wait()

    @pl.loop(0, CHUNKS - 1)
    def _(c):
        chunk_work(c)
        near_chunk(c)

    chunk_work(CHUNKS - 1)

    rt_copy.wait()
    ridx = ri[0:1, :]
    s_id = lax.broadcasted_iota(jnp.int32, (4 * SKEL, SKEL), 0)
    pts = jnp.zeros((ROWS, SKEL), F32)
    wgt = jnp.zeros((RHS, 128), F32)
    rows = pl.ds(pl.multiple_of(half * 128, 128), 128)
    for l in range(0, LEAVES, 4):
        hot = jnp.where(s_id == ridx - l * SKEL, 1.0, 0.0).astype(BF16)
        four = jnp.concatenate([skel_o[l + e] for e in range(4)], axis=1)
        lift = jnp.concatenate([rt[l + e, rows, :] for e in range(4)], axis=1)
        pts = pts + jnp.dot(four, hot, preferred_element_type=F32)
        wgt = wgt + lax.dot_general(four[DIM:RAW], lift, NT, preferred_element_type=F32)
    mine = jnp.where(half == 0, pts[:, :128], pts[:, 128:])

    @pl.when(sender)
    def _():
        rbuf[cx, cz] = jnp.concatenate([mine[:DIM], wgt, mine[RAW:]], axis=0).astype(BF16)

    def root_z(d):
        to = leaf_id(lax.rem(cz + d, 8), cx, core)
        ref = rbuf.at[cx, cz]
        return remote(ref, ref, z_send.at[d - 1], z_recv.at[d - 1], to, b)

    def root_z_wait(d):
        src = lax.rem(cz + 8 - d, 8)
        ref = rbuf.at[cx, src]
        return remote(ref, ref, z_send.at[d - 1], z_recv.at[d - 1], leaf_id(src, cx, core), b)

    def root_x(d):
        to = leaf_id(cz, lax.rem(cx + d, 4), core)
        ref = rbuf.at[cx]
        return remote(ref, ref, x_send.at[d - 1], x_recv.at[d - 1], to, b)

    def root_x_wait(d):
        src = lax.rem(cx + 4 - d, 4)
        ref = rbuf.at[src]
        return remote(ref, ref, x_send.at[d - 1], x_recv.at[d - 1], leaf_id(cz, src, core), b)

    def root_c(d):
        ref = rbuf.at[lax.rem(cx + 4 - d, 4)]
        return remote(ref, ref, c_send.at[d], c_recv.at[d], leaf_id(cz, cx, 1 - core), b)

    @pl.when(sender)
    def _():
        for d in range(1, 8):
            root_z(d).start()

    for h in range(2):
        v = pts[:, h * 128:(h + 1) * 128]
        rts[h * 128:(h + 1) * 128, :] = to_rows(v[:DIM], v[RAW:])

    near_chunk(CHUNKS - 1)

    wlane = lax.broadcasted_iota(jnp.int32, (RHS, 128), 1)
    for k, step in enumerate(STEPS):
        exists = (o + step >= 0) & (o + step < OWNERS)

        @pl.when(exists)
        def _():
            for c in range(CHUNKS):
                far_wait(c, k).wait_recv()

            @pl.loop(0, 8, unroll=8)
            def _(q):
                v = fin[k, q]
                even = k * 16 + 2 * q
                rows = to_rows(v[:DIM], v[RAW:])
                fs[even] = rows[:64]
                fs[even + 1] = rows[64:]
                w = v[DIM:RAW].astype(F32)
                left = jnp.where(wlane < 64, w, 0.0)
                right = jnp.where(wlane < 64, 0.0, w)
                wl[even] = left
                wr[even] = pltpu.roll(left, 64, axis=1)
                wl[even + 1] = pltpu.roll(right, 64, axis=1)
                wr[even + 1] = right

        @pl.when(jnp.logical_not(exists))
        def _():
            @pl.loop(k * 16, k * 16 + 16)
            def _(e):
                fs[e] = jnp.zeros((64, 128), BF16)
                wl[e] = jnp.zeros((RHS, 128), F32)
                wr[e] = jnp.zeros((RHS, 128), F32)

    lists = fl_v[...]

    def named(u):
        f = fl_s[0, u]
        owner = f // LEAVES
        step = owner - o
        at = (step + 2 - jnp.where(step > 0, 1, 0)) * LEAVES + f - owner * LEAVES
        hit = jnp.max(jnp.where(lists == f, 1.0, 0.0), axis=1, keepdims=True)
        return jnp.clip(at, 0, 63), hit * jnp.where(step == 0, 0.0, 1.0)

    for v in range(PAIRS):
        at0, hit0 = named(2 * v)
        at1, hit1 = named(2 * v + 1)
        sall[v * 128:v * 128 + 64, :] = fs[at0]
        sall[v * 128 + 64:v * 128 + 128, :] = fs[at1]
        wall[:, v * 128:(v + 1) * 128] = wl[at0] + wr[at1]
        mask[:, v * 128:(v + 1) * 128] = jnp.where(wlane < 64, hit0, hit1)

    def far_range(lo, hi):
        @pl.loop(lo, hi, step=2)
        def _(l):
            t = jnp.concatenate([skel_o[l], skel_o[l + 1]], axis=1)
            w0 = (wall[...] * mask[pl.ds(l, 1), :]).astype(BF16)
            w1 = (wall[...] * mask[pl.ds(l + 1, 1), :]).astype(BF16)
            x = jnp.dot(sall[:, :ROWS], t, preferred_element_type=F32)
            p = jnp.exp(x).astype(BF16)
            farsum[l] = jnp.dot(w0, p[:, :SKEL], preferred_element_type=F32)
            farsum[l + 1] = jnp.dot(w1, p[:, SKEL:], preferred_element_type=F32)

    @pl.when(sender)
    def _():
        for d in range(1, 8):
            root_z_wait(d).wait_recv()
        for d in range(1, 4):
            root_x(d).start()
        root_c(0).start()

    def scatter_copy(c, d):
        to = lax.rem(b + d, BLKS)
        return remote(part.at[to, pl.ds(c * QUAD, QUAD)], land.at[d - 1, pl.ds(c * QUAD, QUAD)],
                      s_send.at[c, d - 1], s_recv.at[c, d - 1], o, to)

    def far_down(c):
        for l in range(c * QUAD, (c + 1) * QUAD):
            total = near_o[l] + jnp.dot(farsum[l].astype(BF16), li[l], preferred_element_type=F32)
            total = total.astype(BF16)
            for d in range(BLKS):
                part[d, l] = total[:, d * 128:(d + 1) * 128]
        for d in (2, 1, 3):
            scatter_copy(c, d).start()

    far_range(0, FAR_A)
    @pl.when(sender)
    def _():
        for d in range(1, 4):
            root_x_wait(d).wait_recv()
            root_c(d).start()

    far_range(FAR_A, FAR_B)
    for c in range(FAR_B // QUAD):
        far_down(c)

    @pl.when(jnp.logical_not(sender))
    def _():
        for d in range(4):
            root_c(d).wait_recv()

    targets = rts[:, :ROWS]

    def root_group(i, acc):
        cols = []
        wgts = []
        for e in range(4):
            x = i // 2
            z = (i - 2 * x) * 4 + e
            p = leaf_id(z, x, parity)
            v = rbuf[x, z]
            cols.append(v)
            wgts.append(jnp.where(jnp.abs(p - o) > 2, v[DIM:RAW].astype(F32), 0.0).astype(BF16))
        xt = jnp.dot(targets, jnp.concatenate(cols, axis=1), preferred_element_type=F32)
        pt = jnp.exp(xt).astype(BF16)
        w = jnp.concatenate(wgts, axis=1)
        return acc + lax.dot_general(w, pt, NT, preferred_element_type=F32)

    rf = lax.fori_loop(0, 8, root_group, jnp.zeros((RHS, SKEL), F32), unroll=4).astype(BF16)

    rfs[b] = rf

    def root_sum(d):
        return remote(rfs.at[b], rfs.at[b], r_send.at[d - 1], r_recv.at[d - 1], o, lax.rem(b + d, BLKS))

    for d in range(1, BLKS):
        root_sum(d).start()
    far_range(FAR_B, LEAVES)
    for c in range(FAR_B // QUAD, QUADS):
        far_down(c)

    for d in range(1, BLKS):
        root_sum(d).wait_recv()
    field = rfs[0].astype(F32)
    for d in range(1, BLKS):
        field = field + rfs[d].astype(F32)
    field = field.astype(BF16)
    mine = pl.ds(pl.multiple_of(b * 128, 128), 128)
    for c in range(QUADS):
        group = range(c * QUAD, (c + 1) * QUAD)
        lifted = [jnp.dot(field, rt[l], preferred_element_type=F32).astype(BF16) for l in group]
        for d in range(1, BLKS):
            scatter_copy(c, d).wait_recv()
        for l, v in zip(group, lifted):
            total = jnp.dot(v, li[l, :, mine], preferred_element_type=F32)
            total = total + part[b, l].astype(F32)
            for d in range(BLKS - 1):
                total = total + land[d, l].astype(F32)
            out[l] = total

    @pl.when(has_high)
    def _():
        h_up.wait_send()

    @pl.when(has_low)
    def _():
        h_down.wait_send()

    for c in range(CHUNKS):
        for k, step in enumerate(STEPS):
            @pl.when((o + step >= 0) & (o + step < OWNERS))
            def _():
                far_copy(c, k).wait_send()
        for d in (1, 2, 3):
            gather_copy(c, d).wait_send()

    for d in range(1, BLKS):
        root_sum(d).wait_send()
        for c in range(QUADS):
            scatter_copy(c, d).wait_send()

    @pl.when(sender)
    def _():
        for d in range(1, 8):
            root_z(d).wait_send()
        for d in range(1, 4):
            root_x(d).wait_send()
        for d in range(4):
            root_c(d).wait_send()


def on_device(points, charges, leaf_interp, root_interp, skeleton_index, root_index, near_list, far_list, far_count):
    vmem = pl.BlockSpec(memory_space=pltpu.VMEM)
    smem = pl.BlockSpec(memory_space=pltpu.SMEM)
    hbm = pl.BlockSpec(memory_space=pl.ANY)
    dma = pltpu.SemaphoreType.DMA

    out = pl.pallas_call(
        potential_kernel,
        out_shape=jax.ShapeDtypeStruct((LEAVES, RHS, PTS), F32),
        in_specs=[hbm, hbm, smem, smem, vmem, vmem, vmem, hbm, hbm],
        out_specs=vmem,
        scratch_shapes=[
            pltpu.VMEM((DIM, LEAVES, PTS), BF16),
            pltpu.VMEM((RHS, LEAVES, PTS), BF16),
            pltpu.VMEM((LEAVES, RAW, PTS), BF16),
            pltpu.VMEM((BLKS, LEAVES, ROWS, PTS), BF16),
            pltpu.VMEM((2, HALO, RAW, PTS), BF16),
            pltpu.VMEM((2 * HALO + LEAVES, 128, 128), BF16),
            pltpu.VMEM((2 * HALO + LEAVES, RHS, 128), BF16),
            pltpu.VMEM((LEAVES, SKEL, BLKS * PTS), BF16),
            pltpu.VMEM((LEAVES, SKEL, SKEL), BF16),
            pltpu.VMEM((8, ROWS, 128), BF16),
            pltpu.VMEM((4, 8, ROWS, 128), BF16),
            pltpu.VMEM((4, 8, ROWS, 128), BF16),
            pltpu.VMEM((LEAVES, RHS, BLKS * PTS), F32),
            pltpu.VMEM((LEAVES, ROWS, SKEL), BF16),
            pltpu.VMEM((64, 64, 128), BF16),
            pltpu.VMEM((64, RHS, 128), F32),
            pltpu.VMEM((64, RHS, 128), F32),
            pltpu.VMEM((SKEL, 128), BF16),
            pltpu.VMEM((PAIRS * 128, 128), BF16),
            pltpu.VMEM((RHS, PAIRS * 128), F32),
            pltpu.VMEM((LEAVES, PAIRS * 128), F32),
            pltpu.VMEM((LEAVES, RHS, SKEL), F32),
            pltpu.VMEM((BLKS, LEAVES, RHS, PTS), BF16),
            pltpu.VMEM((BLKS - 1, LEAVES, RHS, PTS), BF16),
            pltpu.VMEM((BLKS, RHS, SKEL), BF16),
            dma, dma, dma, dma,
            dma((CHUNKS, 3)), dma((CHUNKS, 3)),
            dma((2,)), dma((2,)),
            dma((CHUNKS, 4)), dma((CHUNKS, 4)),
            dma((7,)), dma((7,)), dma((3,)), dma((3,)), dma((4,)), dma((4,)),
            dma((QUADS, 3)), dma((QUADS, 3)), dma((3,)), dma((3,)),
        ],
        compiler_params=pltpu.CompilerParams(
            collective_id=0, has_side_effects=True, vmem_limit_bytes=VMEM_LIMIT),
    )(points, charges, near_list, far_list, far_list, skeleton_index, root_index, leaf_interp, root_interp)
    return jnp.transpose(out, (1, 0, 2))


def solution(mesh):
    placed = (
        P(None, "leaf", "blk"),
        P(None, "leaf", "blk"),
        P("leaf", None, None),
        P("leaf", None, None),
        P("leaf", None),
        P("leaf", None),
        P("leaf", None),
        P("leaf", None),
        P("leaf"),
    )
    return jax.shard_map(
        on_device, mesh=mesh, in_specs=placed, out_specs=P(None, "leaf", "blk"), check_vma=False
    )
```

```python
import jax
import jax.numpy as jnp
from jax import lax
from jax.experimental import pallas as pl
from jax.experimental.pallas import tpu as pltpu
from jax.sharding import PartitionSpec as P

MESH = pl.DeviceIdType.MESH
F32 = jnp.float32
BF16 = jnp.bfloat16
NT = (((1,), (1,)), ((), ()))

DIM = 64
RHS = 16
RAW = DIM + RHS
ROWS = 96
LEAVES = 16
PTS = 128
BLKS = 4
SKEL = 256
HALO = 8
NEAR = 10
FAR = 32
OWNERS = 64
CHUNKS = 8
CHUNK = LEAVES // CHUNKS
QUADS = 4
QUAD = LEAVES // QUADS
STEPS = (-2, -1, 1, 2)
PAIRS = FAR // 2
FAR_A = 10
FAR_B = 12
VMEM_LIMIT = 58 * 2**20


def aug_rows(points):
    p = points.astype(F32)
    n = -0.5 * jnp.sum(p * p, axis=0, keepdims=True)
    hi = n.astype(BF16).astype(F32)
    rest = n - hi
    mid = rest.astype(BF16).astype(F32)
    low = rest - mid
    row = lax.broadcasted_iota(jnp.int32, (16, n.shape[1]), 0)
    out = jnp.where(row == 0, hi, jnp.where(row == 1, mid, jnp.where(row == 2, low, 0.0)))
    out = jnp.where((row >= 4) & (row < 7), 1.0, out)
    return out.astype(BF16)


def to_rows(points, aug):
    a = aug.astype(F32)[:8]
    swapped = jnp.concatenate([a[4:], a[:4]], axis=0)
    z16 = jnp.zeros((16, 128), F32)
    z40 = jnp.zeros((40, 128), F32)
    full = jnp.concatenate([points.astype(F32), z16, swapped, z40], axis=0)
    return full.T.astype(BF16)


def leaf_id(z, x, c):
    return (z * 4 + x) * 2 + c


def potential_kernel(
    points_hbm, charges_hbm, nl, fl_s, fl_v, si, ri, li_hbm, rt_hbm,
    out,
    points, charges, own, gath, halo, srow, swgt, li, rt, fout, fin, rbuf,
    near_o, skel_o, fs, wl, wr, rts, sall, wall, mask, farsum, part, land, rfs,
    p_sem, q_sem, li_sem, rt_sem, y_send, y_recv, h_send, h_recv,
    far_send, far_recv, z_send, z_recv, x_send, x_recv, c_send, c_recv, s_send, s_recv, r_send, r_recv,
):
    o = lax.axis_index("leaf")
    b = lax.axis_index("blk")
    core = lax.rem(o, 2)
    cx = lax.rem(o // 2, 4)
    cz = o // 8
    up = lax.rem(b + 1, BLKS)
    down = lax.rem(b + BLKS - 1, BLKS)
    half = lax.rem(b, 2)
    parity = b // 2
    sender = core == parity

    li_copy = pltpu.make_async_copy(li_hbm, li, li_sem)
    rt_copy = pltpu.make_async_copy(rt_hbm, rt, rt_sem)
    p_copy = pltpu.make_async_copy(points_hbm, points, p_sem)
    q_copy = pltpu.make_async_copy(charges_hbm, charges, q_sem)
    p_copy.start()
    q_copy.start()

    barrier = pltpu.get_barrier_semaphore()

    def greet(leaf, blk):
        pl.semaphore_signal(barrier, inc=1, device_id=(leaf, blk), device_id_type=MESH)

    greet(o, up)
    greet(o, down)
    for d in range(1, 8):
        greet(leaf_id(lax.rem(cz + d, 8), cx, core), b)
    for d in range(1, 4):
        greet(leaf_id(cz, lax.rem(cx + d, 4), core), b)
    greet(leaf_id(cz, cx, 1 - core), b)
    greet(o, lax.rem(b + 2, BLKS))
    for step in STEPS:
        @pl.when((o + step >= 0) & (o + step < OWNERS))
        def _():
            greet(o + step, b)

    p_copy.wait()
    q_copy.wait()
    li_copy.start()
    rt_copy.start()
    for h in range(2):
        for g in range(DIM // 16):
            v = points[g * 16:(g + 1) * 16, h * 8:(h + 1) * 8, :].astype(F32)
            own[h * 8:(h + 1) * 8, g * 16:(g + 1) * 16, :] = jnp.swapaxes(v, 0, 1).astype(BF16)
        v = charges[:, h * 8:(h + 1) * 8, :].astype(F32)
        own[h * 8:(h + 1) * 8, DIM:RAW, :] = jnp.swapaxes(v, 0, 1).astype(BF16)

    pl.semaphore_wait(barrier, 14 + jnp.minimum(o, 2) + jnp.minimum(OWNERS - 1 - o, 2))

    def remote(src, dst, ssem, rsem, leaf, blk):
        return pltpu.make_async_remote_copy(
            src_ref=src, dst_ref=dst, send_sem=ssem, recv_sem=rsem,
            device_id=(leaf, blk), device_id_type=MESH)

    has_low = o > 0
    has_high = o < OWNERS - 1
    h_up = remote(own.at[pl.ds(LEAVES - HALO, HALO)], halo.at[0], h_send.at[0], h_recv.at[0], o + 1, b)
    h_down = remote(own.at[pl.ds(0, HALO)], halo.at[1], h_send.at[1], h_recv.at[1], o - 1, b)

    @pl.when(has_high)
    def _():
        h_up.start()

    @pl.when(has_low)
    def _():
        h_down.start()

    def leaves(c):
        return pl.ds(c * CHUNK, CHUNK)

    def gather_copy(c, d):
        return remote(own.at[leaves(c)], gath.at[b, leaves(c), pl.ds(0, RAW)],
                      y_send.at[c, d - 1], y_recv.at[c, d - 1], o, lax.rem(b + d, BLKS))

    def leaves(c):
        return pl.ds(c * CHUNK, CHUNK)

    for c in range(CHUNKS):
        for d in (2, 1, 3):
            gather_copy(c, d).start()

    def take_halo(side, at):
        @pl.loop(0, HALO, unroll=8)
        def _(l):
            raw = halo[side, l]
            srow[at + l] = to_rows(raw[:DIM], aug_rows(raw[:DIM]))
            swgt[at + l] = raw[DIM:]

    def no_halo(at):
        @pl.loop(0, HALO)
        def _(l):
            srow[at + l] = jnp.zeros((128, 128), BF16)
            swgt[at + l] = jnp.zeros((RHS, 128), BF16)

    near_base = HALO - o * LEAVES

    def near_leaf(l):
        ids = [jnp.clip(nl[l, j] + near_base, 0, 2 * HALO + LEAVES - 1) for j in range(NEAR)]
        s = jnp.concatenate([srow[i] for i in ids], axis=0)[:, :ROWS]
        w = jnp.concatenate([swgt[i] for i in ids], axis=1)
        t = jnp.concatenate([gath[k, l] for k in range(BLKS)], axis=1)
        x = jnp.dot(s, t, preferred_element_type=F32)
        p = jnp.exp(x).astype(BF16)
        near_o[l] = jnp.dot(w, p, preferred_element_type=F32)

    def near_chunk(c):
        @pl.loop(0, CHUNK, unroll=2)
        def _(i):
            near_leaf(c * CHUNK + i)

    def skeleton_leaf(l):
        t = jnp.concatenate([gath[k, l] for k in range(BLKS)], axis=1)
        idx = si[pl.ds(l, 1), :]
        m = lax.broadcasted_iota(jnp.int32, (BLKS * PTS, SKEL), 0)
        hot = jnp.where(m == idx, 1.0, 0.0).astype(BF16)
        nat = jnp.dot(t, hot, preferred_element_type=F32)
        wgt = lax.dot_general(t[DIM:RAW], li[l], NT, preferred_element_type=F32)
        skel_o[l] = jnp.concatenate([nat[:DIM], wgt, nat[RAW:]], axis=0).astype(BF16)

    lane = lax.broadcasted_iota(jnp.int32, (ROWS, 128), 1)

    def quarter(l):
        v = skel_o[l].astype(F32)
        return jnp.where(parity == 0, v[:, :128], v[:, 128:])

    def far_pair(q):
        a = quarter(2 * q)
        c = quarter(2 * q + 1)
        a = jnp.where(half == 0, a, pltpu.roll(a, 64, axis=1))
        c = jnp.where(half == 1, c, pltpu.roll(c, 64, axis=1))
        fout[q] = jnp.where(lane < 64, a, c).astype(BF16)

    def far_copy(c, k):
        part = pl.ds(c * (CHUNK // 2), CHUNK // 2)
        return remote(fout.at[part], fin.at[3 - k, part], far_send.at[c, k], far_recv.at[c, 3 - k],
                      o + STEPS[k], b)

    def far_wait(c, k):
        part = pl.ds(c * (CHUNK // 2), CHUNK // 2)
        return remote(fout.at[part], fin.at[k, part], far_send.at[c, k], far_recv.at[c, k],
                      o + STEPS[k], b)

    opp = lax.rem(b + 2, BLKS)

    def chunk_work(c, with_near):
        for d in (2, 1, 3):
            gather_copy(c, d).wait_recv()

        for i in range(CHUNK):
            l = c * CHUNK + i
            gath[up, l, RAW:ROWS, :] = aug_rows(gath[up, l, 0:DIM, :])
            gath[down, l, RAW:ROWS, :] = aug_rows(gath[down, l, 0:DIM, :])
            gath[opp, l, RAW:ROWS, :] = aug_rows(gath[opp, l, 0:DIM, :])
            skeleton_leaf(l)
        for i in range(CHUNK // 2):
            far_pair(c * (CHUNK // 2) + i)
        if with_near:
            for i in range(CHUNK):
                near_leaf(c * CHUNK + i)

        for k, step in enumerate(STEPS):
            @pl.when((o + step >= 0) & (o + step < OWNERS))
            def _():
                far_copy(c, k).start()

    def halo_rows():
        @pl.when(has_low)
        def _():
            h_up.wait_recv()
            take_halo(0, 0)

        @pl.when(jnp.logical_not(has_low))
        def _():
            no_halo(0)

        @pl.when(has_high)
        def _():
            h_down.wait_recv()
            take_halo(1, HALO + LEAVES)

        @pl.when(jnp.logical_not(has_high))
        def _():
            no_halo(HALO + LEAVES)

    @pl.loop(0, LEAVES, unroll=4)
    def _(l):
        raw = own[l]
        aug = aug_rows(raw[:DIM])
        gath[b, l, 0:RAW, :] = raw
        gath[b, l, RAW:ROWS, :] = aug
        srow[HALO + l] = to_rows(raw[:DIM], aug)
        swgt[HALO + l] = raw[DIM:]

    halo_rows()
    li_copy.wait()

    @pl.loop(0, CHUNKS - 1)
    def _(c):
        chunk_work(c, True)

    chunk_work(CHUNKS - 1, False)

    rt_copy.wait()
    ridx = ri[0:1, :]
    s_id = lax.broadcasted_iota(jnp.int32, (4 * SKEL, SKEL), 0)
    pts = jnp.zeros((ROWS, SKEL), F32)
    wgt = jnp.zeros((RHS, 128), F32)
    rows = pl.ds(pl.multiple_of(half * 128, 128), 128)
    for l in range(0, LEAVES, 4):
        hot = jnp.where(s_id == ridx - l * SKEL, 1.0, 0.0).astype(BF16)
        four = jnp.concatenate([skel_o[l + e] for e in range(4)], axis=1)
        lift = jnp.concatenate([rt[l + e, rows, :] for e in range(4)], axis=1)
        pts = pts + jnp.dot(four, hot, preferred_element_type=F32)
        wgt = wgt + lax.dot_general(four[DIM:RAW], lift, NT, preferred_element_type=F32)
    mine = jnp.where(half == 0, pts[:, :128], pts[:, 128:])

    @pl.when(sender)
    def _():
        rbuf[cx, cz] = jnp.concatenate([mine[:DIM], wgt, mine[RAW:]], axis=0).astype(BF16)

    def root_z(d):
        to = leaf_id(lax.rem(cz + d, 8), cx, core)
        ref = rbuf.at[cx, cz]
        return remote(ref, ref, z_send.at[d - 1], z_recv.at[d - 1], to, b)

    def root_z_wait(d):
        src = lax.rem(cz + 8 - d, 8)
        ref = rbuf.at[cx, src]
        return remote(ref, ref, z_send.at[d - 1], z_recv.at[d - 1], leaf_id(src, cx, core), b)

    def root_x(d):
        to = leaf_id(cz, lax.rem(cx + d, 4), core)
        ref = rbuf.at[cx]
        return remote(ref, ref, x_send.at[d - 1], x_recv.at[d - 1], to, b)

    def root_x_wait(d):
        src = lax.rem(cx + 4 - d, 4)
        ref = rbuf.at[src]
        return remote(ref, ref, x_send.at[d - 1], x_recv.at[d - 1], leaf_id(cz, src, core), b)

    def root_c(d):
        ref = rbuf.at[lax.rem(cx + 4 - d, 4)]
        return remote(ref, ref, c_send.at[d], c_recv.at[d], leaf_id(cz, cx, 1 - core), b)

    @pl.when(sender)
    def _():
        for d in range(1, 8):
            root_z(d).start()

    for h in range(2):
        v = pts[:, h * 128:(h + 1) * 128]
        rts[h * 128:(h + 1) * 128, :] = to_rows(v[:DIM], v[RAW:])

    near_chunk(CHUNKS - 1)

    wlane = lax.broadcasted_iota(jnp.int32, (RHS, 128), 1)
    for k, step in enumerate(STEPS):
        exists = (o + step >= 0) & (o + step < OWNERS)

        @pl.when(exists)
        def _():
            for c in range(CHUNKS):
                far_wait(c, k).wait_recv()

            @pl.loop(0, 8, unroll=8)
            def _(q):
                v = fin[k, q]
                even = k * 16 + 2 * q
                rows = to_rows(v[:DIM], v[RAW:])
                fs[even] = rows[:64]
                fs[even + 1] = rows[64:]
                w = v[DIM:RAW].astype(F32)
                left = jnp.where(wlane < 64, w, 0.0)
                right = jnp.where(wlane < 64, 0.0, w)
                wl[even] = left
                wr[even] = pltpu.roll(left, 64, axis=1)
                wl[even + 1] = pltpu.roll(right, 64, axis=1)
                wr[even + 1] = right

        @pl.when(jnp.logical_not(exists))
        def _():
            @pl.loop(k * 16, k * 16 + 16)
            def _(e):
                fs[e] = jnp.zeros((64, 128), BF16)
                wl[e] = jnp.zeros((RHS, 128), F32)
                wr[e] = jnp.zeros((RHS, 128), F32)

    lists = fl_v[...]

    def named(u):
        f = fl_s[0, u]
        owner = f // LEAVES
        step = owner - o
        at = (step + 2 - jnp.where(step > 0, 1, 0)) * LEAVES + f - owner * LEAVES
        hit = jnp.max(jnp.where(lists == f, 1.0, 0.0), axis=1, keepdims=True)
        return jnp.clip(at, 0, 63), hit * jnp.where(step == 0, 0.0, 1.0)

    for v in range(PAIRS):
        at0, hit0 = named(2 * v)
        at1, hit1 = named(2 * v + 1)
        sall[v * 128:v * 128 + 64, :] = fs[at0]
        sall[v * 128 + 64:v * 128 + 128, :] = fs[at1]
        wall[:, v * 128:(v + 1) * 128] = wl[at0] + wr[at1]
        mask[:, v * 128:(v + 1) * 128] = jnp.where(wlane < 64, hit0, hit1)

    def far_range(lo, hi):
        @pl.loop(lo, hi, step=2)
        def _(l):
            t = jnp.concatenate([skel_o[l], skel_o[l + 1]], axis=1)
            w0 = (wall[...] * mask[pl.ds(l, 1), :]).astype(BF16)
            w1 = (wall[...] * mask[pl.ds(l + 1, 1), :]).astype(BF16)
            x = jnp.dot(sall[:, :ROWS], t, preferred_element_type=F32)
            p = jnp.exp(x).astype(BF16)
            farsum[l] = jnp.dot(w0, p[:, :SKEL], preferred_element_type=F32)
            farsum[l + 1] = jnp.dot(w1, p[:, SKEL:], preferred_element_type=F32)

    @pl.when(sender)
    def _():
        for d in range(1, 8):
            root_z_wait(d).wait_recv()
        for d in range(1, 4):
            root_x(d).start()
        root_c(0).start()

    def scatter_copy(c, d):
        to = lax.rem(b + d, BLKS)
        return remote(part.at[to, pl.ds(c * QUAD, QUAD)], land.at[d - 1, pl.ds(c * QUAD, QUAD)],
                      s_send.at[c, d - 1], s_recv.at[c, d - 1], o, to)

    def far_down(c):
        for l in range(c * QUAD, (c + 1) * QUAD):
            total = near_o[l] + jnp.dot(farsum[l].astype(BF16), li[l], preferred_element_type=F32)
            total = total.astype(BF16)
            for d in range(BLKS):
                part[d, l] = total[:, d * 128:(d + 1) * 128]
        for d in (2, 1, 3):
            scatter_copy(c, d).start()

    far_range(0, FAR_A)
    @pl.when(sender)
    def _():
        for d in range(1, 4):
            root_x_wait(d).wait_recv()
            root_c(d).start()

    far_range(FAR_A, FAR_B)
    for c in range(FAR_B // QUAD):
        far_down(c)

    @pl.when(jnp.logical_not(sender))
    def _():
        for d in range(4):
            root_c(d).wait_recv()

    targets = rts[:, :ROWS]

    def root_group(i, acc):
        cols = []
        wgts = []
        for e in range(4):
            x = i // 2
            z = (i - 2 * x) * 4 + e
            p = leaf_id(z, x, parity)
            v = rbuf[x, z]
            cols.append(v)
            wgts.append(jnp.where(jnp.abs(p - o) > 2, v[DIM:RAW].astype(F32), 0.0).astype(BF16))
        xt = jnp.dot(targets, jnp.concatenate(cols, axis=1), preferred_element_type=F32)
        pt = jnp.exp(xt).astype(BF16)
        w = jnp.concatenate(wgts, axis=1)
        return acc + lax.dot_general(w, pt, NT, preferred_element_type=F32)

    rf = lax.fori_loop(0, 8, root_group, jnp.zeros((RHS, SKEL), F32), unroll=4).astype(BF16)

    rfs[b] = rf

    def root_sum(d):
        return remote(rfs.at[b], rfs.at[b], r_send.at[d - 1], r_recv.at[d - 1], o, lax.rem(b + d, BLKS))

    for d in range(1, BLKS):
        root_sum(d).start()
    far_range(FAR_B, LEAVES)
    for c in range(FAR_B // QUAD, QUADS):
        far_down(c)

    for d in range(1, BLKS):
        root_sum(d).wait_recv()
    field = rfs[0].astype(F32)
    for d in range(1, BLKS):
        field = field + rfs[d].astype(F32)
    field = field.astype(BF16)
    mine = pl.ds(pl.multiple_of(b * 128, 128), 128)
    for c in range(QUADS):
        group = range(c * QUAD, (c + 1) * QUAD)
        lifted = [jnp.dot(field, rt[l], preferred_element_type=F32).astype(BF16) for l in group]
        for d in range(1, BLKS):
            scatter_copy(c, d).wait_recv()
        for l, v in zip(group, lifted):
            total = jnp.dot(v, li[l, :, mine], preferred_element_type=F32)
            total = total + part[b, l].astype(F32)
            for d in range(BLKS - 1):
                total = total + land[d, l].astype(F32)
            out[l] = total

    @pl.when(has_high)
    def _():
        h_up.wait_send()

    @pl.when(has_low)
    def _():
        h_down.wait_send()

    for c in range(CHUNKS):
        for k, step in enumerate(STEPS):
            @pl.when((o + step >= 0) & (o + step < OWNERS))
            def _():
                far_copy(c, k).wait_send()
        for d in (1, 2, 3):
            gather_copy(c, d).wait_send()

    for d in range(1, BLKS):
        root_sum(d).wait_send()
        for c in range(QUADS):
            scatter_copy(c, d).wait_send()

    @pl.when(sender)
    def _():
        for d in range(1, 8):
            root_z(d).wait_send()
        for d in range(1, 4):
            root_x(d).wait_send()
        for d in range(4):
            root_c(d).wait_send()


def on_device(points, charges, leaf_interp, root_interp, skeleton_index, root_index, near_list, far_list, far_count):
    vmem = pl.BlockSpec(memory_space=pltpu.VMEM)
    smem = pl.BlockSpec(memory_space=pltpu.SMEM)
    hbm = pl.BlockSpec(memory_space=pl.ANY)
    dma = pltpu.SemaphoreType.DMA

    out = pl.pallas_call(
        potential_kernel,
        out_shape=jax.ShapeDtypeStruct((LEAVES, RHS, PTS), F32),
        in_specs=[hbm, hbm, smem, smem, vmem, vmem, vmem, hbm, hbm],
        out_specs=vmem,
        scratch_shapes=[
            pltpu.VMEM((DIM, LEAVES, PTS), BF16),
            pltpu.VMEM((RHS, LEAVES, PTS), BF16),
            pltpu.VMEM((LEAVES, RAW, PTS), BF16),
            pltpu.VMEM((BLKS, LEAVES, ROWS, PTS), BF16),
            pltpu.VMEM((2, HALO, RAW, PTS), BF16),
            pltpu.VMEM((2 * HALO + LEAVES, 128, 128), BF16),
            pltpu.VMEM((2 * HALO + LEAVES, RHS, 128), BF16),
            pltpu.VMEM((LEAVES, SKEL, BLKS * PTS), BF16),
            pltpu.VMEM((LEAVES, SKEL, SKEL), BF16),
            pltpu.VMEM((8, ROWS, 128), BF16),
            pltpu.VMEM((4, 8, ROWS, 128), BF16),
            pltpu.VMEM((4, 8, ROWS, 128), BF16),
            pltpu.VMEM((LEAVES, RHS, BLKS * PTS), F32),
            pltpu.VMEM((LEAVES, ROWS, SKEL), BF16),
            pltpu.VMEM((64, 64, 128), BF16),
            pltpu.VMEM((64, RHS, 128), F32),
            pltpu.VMEM((64, RHS, 128), F32),
            pltpu.VMEM((SKEL, 128), BF16),
            pltpu.VMEM((PAIRS * 128, 128), BF16),
            pltpu.VMEM((RHS, PAIRS * 128), F32),
            pltpu.VMEM((LEAVES, PAIRS * 128), F32),
            pltpu.VMEM((LEAVES, RHS, SKEL), F32),
            pltpu.VMEM((BLKS, LEAVES, RHS, PTS), BF16),
            pltpu.VMEM((BLKS - 1, LEAVES, RHS, PTS), BF16),
            pltpu.VMEM((BLKS, RHS, SKEL), BF16),
            dma, dma, dma, dma,
            dma((CHUNKS, 3)), dma((CHUNKS, 3)),
            dma((2,)), dma((2,)),
            dma((CHUNKS, 4)), dma((CHUNKS, 4)),
            dma((7,)), dma((7,)), dma((3,)), dma((3,)), dma((4,)), dma((4,)),
            dma((QUADS, 3)), dma((QUADS, 3)), dma((3,)), dma((3,)),
        ],
        compiler_params=pltpu.CompilerParams(
            collective_id=0, has_side_effects=True, vmem_limit_bytes=VMEM_LIMIT),
    )(points, charges, near_list, far_list, far_list, skeleton_index, root_index, leaf_interp, root_interp)
    return jnp.transpose(out, (1, 0, 2))


def solution(mesh):
    placed = (
        P(None, "leaf", "blk"),
        P(None, "leaf", "blk"),
        P("leaf", None, None),
        P("leaf", None, None),
        P("leaf", None),
        P("leaf", None),
        P("leaf", None),
        P("leaf", None),
        P("leaf"),
    )
    return jax.shard_map(
        on_device, mesh=mesh, in_specs=placed, out_specs=P(None, "leaf", "blk"), check_vma=False
    )
```

```python
import jax
import jax.numpy as jnp
from jax import lax
from jax.experimental import pallas as pl
from jax.experimental.pallas import tpu as pltpu
from jax.sharding import PartitionSpec as P

MESH = pl.DeviceIdType.MESH
F32 = jnp.float32
BF16 = jnp.bfloat16
NT = (((1,), (1,)), ((), ()))

DIM = 64
RHS = 16
RAW = DIM + RHS
ROWS = 96
LEAVES = 16
PTS = 128
BLKS = 4
SKEL = 256
HALO = 8
NEAR = 10
FAR = 32
OWNERS = 64
CHUNKS = 8
CHUNK = LEAVES // CHUNKS
QUADS = 4
QUAD = LEAVES // QUADS
STEPS = (-2, -1, 1, 2)
PAIRS = FAR // 2
FAR_A = 10
FAR_B = 12
VMEM_LIMIT = 58 * 2**20


def aug_rows(points):
    p = points.astype(F32)
    n = -0.5 * jnp.sum(p * p, axis=0, keepdims=True)
    hi = n.astype(BF16).astype(F32)
    rest = n - hi
    mid = rest.astype(BF16).astype(F32)
    low = rest - mid
    row = lax.broadcasted_iota(jnp.int32, (16, n.shape[1]), 0)
    out = jnp.where(row == 0, hi, jnp.where(row == 1, mid, jnp.where(row == 2, low, 0.0)))
    out = jnp.where((row >= 4) & (row < 7), 1.0, out)
    return out.astype(BF16)


def to_rows(points, aug):
    a = aug.astype(F32)[:8]
    swapped = jnp.concatenate([a[4:], a[:4]], axis=0)
    z16 = jnp.zeros((16, 128), F32)
    z40 = jnp.zeros((40, 128), F32)
    full = jnp.concatenate([points.astype(F32), z16, swapped, z40], axis=0)
    return full.T.astype(BF16)


def leaf_id(z, x, c):
    return (z * 4 + x) * 2 + c


def potential_kernel(
    points_hbm, charges_hbm, nl, fl_s, fl_v, si, ri, li_hbm, rt_hbm,
    out,
    points, charges, own, gath, halo, srow, swgt, li, rt, fout, fin, rbuf,
    near_o, skel_o, fs, wl, wr, rts, sall, wall, mask, farsum, part, land, rfs,
    p_sem, q_sem, li_sem, rt_sem, y_send, y_recv, h_send, h_recv,
    far_send, far_recv, z_send, z_recv, x_send, x_recv, c_send, c_recv, s_send, s_recv, r_send, r_recv,
):
    o = lax.axis_index("leaf")
    b = lax.axis_index("blk")
    core = lax.rem(o, 2)
    cx = lax.rem(o // 2, 4)
    cz = o // 8
    up = lax.rem(b + 1, BLKS)
    down = lax.rem(b + BLKS - 1, BLKS)
    half = lax.rem(b, 2)
    parity = b // 2
    sender = core == parity

    li_copy = pltpu.make_async_copy(li_hbm, li, li_sem)
    rt_copy = pltpu.make_async_copy(rt_hbm, rt, rt_sem)
    p_copy = pltpu.make_async_copy(points_hbm, points, p_sem)
    q_copy = pltpu.make_async_copy(charges_hbm, charges, q_sem)
    p_copy.start()
    q_copy.start()

    barrier = pltpu.get_barrier_semaphore()

    def greet(leaf, blk):
        pl.semaphore_signal(barrier, inc=1, device_id=(leaf, blk), device_id_type=MESH)

    greet(o, up)
    greet(o, down)
    for d in range(1, 8):
        greet(leaf_id(lax.rem(cz + d, 8), cx, core), b)
    for d in range(1, 4):
        greet(leaf_id(cz, lax.rem(cx + d, 4), core), b)
    greet(leaf_id(cz, cx, 1 - core), b)
    greet(o, lax.rem(b + 2, BLKS))
    for step in STEPS:
        @pl.when((o + step >= 0) & (o + step < OWNERS))
        def _():
            greet(o + step, b)

    p_copy.wait()
    q_copy.wait()
    li_copy.start()
    rt_copy.start()
    for h in range(2):
        for g in range(DIM // 16):
            v = points[g * 16:(g + 1) * 16, h * 8:(h + 1) * 8, :].astype(F32)
            own[h * 8:(h + 1) * 8, g * 16:(g + 1) * 16, :] = jnp.swapaxes(v, 0, 1).astype(BF16)
        v = charges[:, h * 8:(h + 1) * 8, :].astype(F32)
        own[h * 8:(h + 1) * 8, DIM:RAW, :] = jnp.swapaxes(v, 0, 1).astype(BF16)

    pl.semaphore_wait(barrier, 14 + jnp.minimum(o, 2) + jnp.minimum(OWNERS - 1 - o, 2))

    def remote(src, dst, ssem, rsem, leaf, blk):
        return pltpu.make_async_remote_copy(
            src_ref=src, dst_ref=dst, send_sem=ssem, recv_sem=rsem,
            device_id=(leaf, blk), device_id_type=MESH)

    has_low = o > 0
    has_high = o < OWNERS - 1
    h_up = remote(own.at[pl.ds(LEAVES - HALO, HALO)], halo.at[0], h_send.at[0], h_recv.at[0], o + 1, b)
    h_down = remote(own.at[pl.ds(0, HALO)], halo.at[1], h_send.at[1], h_recv.at[1], o - 1, b)

    @pl.when(has_high)
    def _():
        h_up.start()

    @pl.when(has_low)
    def _():
        h_down.start()

    def leaves(c):
        return pl.ds(c * CHUNK, CHUNK)

    def gather_copy(c, d):
        return remote(own.at[leaves(c)], gath.at[b, leaves(c), pl.ds(0, RAW)],
                      y_send.at[c, d - 1], y_recv.at[c, d - 1], o, lax.rem(b + d, BLKS))

    def leaves(c):
        return pl.ds(c * CHUNK, CHUNK)

    for c in range(CHUNKS):
        for d in (2, 1, 3):
            gather_copy(c, d).start()

    def take_halo(side, at):
        @pl.loop(0, HALO, unroll=8)
        def _(l):
            raw = halo[side, l]
            srow[at + l] = to_rows(raw[:DIM], aug_rows(raw[:DIM]))
            swgt[at + l] = raw[DIM:]

    def no_halo(at):
        @pl.loop(0, HALO)
        def _(l):
            srow[at + l] = jnp.zeros((128, 128), BF16)
            swgt[at + l] = jnp.zeros((RHS, 128), BF16)

    near_base = HALO - o * LEAVES

    def near_leaf(l):
        ids = [jnp.clip(nl[l, j] + near_base, 0, 2 * HALO + LEAVES - 1) for j in range(NEAR)]
        s = jnp.concatenate([srow[i] for i in ids], axis=0)[:, :ROWS]
        w = jnp.concatenate([swgt[i] for i in ids], axis=1)
        t = jnp.concatenate([gath[k, l] for k in range(BLKS)], axis=1)
        x = jnp.dot(s, t, preferred_element_type=F32)
        p = jnp.exp(x).astype(BF16)
        near_o[l] = jnp.dot(w, p, preferred_element_type=F32)

    def near_chunk(c):
        @pl.loop(0, CHUNK, unroll=2)
        def _(i):
            near_leaf(c * CHUNK + i)

    def skeleton_leaf(l):
        t = jnp.concatenate([gath[k, l] for k in range(BLKS)], axis=1)
        idx = si[pl.ds(l, 1), :]
        m = lax.broadcasted_iota(jnp.int32, (BLKS * PTS, SKEL), 0)
        hot = jnp.where(m == idx, 1.0, 0.0).astype(BF16)
        nat = jnp.dot(t, hot, preferred_element_type=F32)
        wgt = lax.dot_general(t[DIM:RAW], li[l], NT, preferred_element_type=F32)
        skel_o[l] = jnp.concatenate([nat[:DIM], wgt, nat[RAW:]], axis=0).astype(BF16)

    lane = lax.broadcasted_iota(jnp.int32, (ROWS, 128), 1)

    def quarter(l):
        v = skel_o[l].astype(F32)
        return jnp.where(parity == 0, v[:, :128], v[:, 128:])

    def far_pair(q):
        a = quarter(2 * q)
        c = quarter(2 * q + 1)
        a = jnp.where(half == 0, a, pltpu.roll(a, 64, axis=1))
        c = jnp.where(half == 1, c, pltpu.roll(c, 64, axis=1))
        fout[q] = jnp.where(lane < 64, a, c).astype(BF16)

    def far_copy(c, k):
        part = pl.ds(c * (CHUNK // 2), CHUNK // 2)
        return remote(fout.at[part], fin.at[3 - k, part], far_send.at[c, k], far_recv.at[c, 3 - k],
                      o + STEPS[k], b)

    def far_wait(c, k):
        part = pl.ds(c * (CHUNK // 2), CHUNK // 2)
        return remote(fout.at[part], fin.at[k, part], far_send.at[c, k], far_recv.at[c, k],
                      o + STEPS[k], b)

    opp = lax.rem(b + 2, BLKS)

    def chunk_work(c, with_near):
        for d in (2, 1, 3):
            gather_copy(c, d).wait_recv()

        for i in range(CHUNK):
            l = c * CHUNK + i
            gath[up, l, RAW:ROWS, :] = aug_rows(gath[up, l, 0:DIM, :])
            gath[down, l, RAW:ROWS, :] = aug_rows(gath[down, l, 0:DIM, :])
            gath[opp, l, RAW:ROWS, :] = aug_rows(gath[opp, l, 0:DIM, :])
            skeleton_leaf(l)
        for i in range(CHUNK // 2):
            far_pair(c * (CHUNK // 2) + i)
        if with_near:
            for i in range(CHUNK):
                near_leaf(c * CHUNK + i)

        for k, step in enumerate(STEPS):
            @pl.when((o + step >= 0) & (o + step < OWNERS))
            def _():
                far_copy(c, k).start()

    def halo_rows():
        @pl.when(has_low)
        def _():
            h_up.wait_recv()
            take_halo(0, 0)

        @pl.when(jnp.logical_not(has_low))
        def _():
            no_halo(0)

        @pl.when(has_high)
        def _():
            h_down.wait_recv()
            take_halo(1, HALO + LEAVES)

        @pl.when(jnp.logical_not(has_high))
        def _():
            no_halo(HALO + LEAVES)

    @pl.loop(0, LEAVES, unroll=4)
    def _(l):
        raw = own[l]
        aug = aug_rows(raw[:DIM])
        gath[b, l, 0:RAW, :] = raw
        gath[b, l, RAW:ROWS, :] = aug
        srow[HALO + l] = to_rows(raw[:DIM], aug)
        swgt[HALO + l] = raw[DIM:]

    halo_rows()
    li_copy.wait()

    @pl.loop(0, CHUNKS - 1)
    def _(c):
        chunk_work(c, True)

    chunk_work(CHUNKS - 1, False)

    rt_copy.wait()
    ridx = ri[0:1, :]
    s_id = lax.broadcasted_iota(jnp.int32, (4 * SKEL, SKEL), 0)
    pts = jnp.zeros((ROWS, SKEL), F32)
    wgt = jnp.zeros((RHS, 128), F32)
    rows = pl.ds(pl.multiple_of(half * 128, 128), 128)
    for l in range(0, LEAVES, 4):
        hot = jnp.where(s_id == ridx - l * SKEL, 1.0, 0.0).astype(BF16)
        four = jnp.concatenate([skel_o[l + e] for e in range(4)], axis=1)
        lift = jnp.concatenate([rt[l + e, rows, :] for e in range(4)], axis=1)
        pts = pts + jnp.dot(four, hot, preferred_element_type=F32)
        wgt = wgt + lax.dot_general(four[DIM:RAW], lift, NT, preferred_element_type=F32)
    mine = jnp.where(half == 0, pts[:, :128], pts[:, 128:])

    @pl.when(sender)
    def _():
        rbuf[cx, cz] = jnp.concatenate([mine[:DIM], wgt, mine[RAW:]], axis=0).astype(BF16)

    def root_z(d):
        to = leaf_id(lax.rem(cz + d, 8), cx, core)
        ref = rbuf.at[cx, cz]
        return remote(ref, ref, z_send.at[d - 1], z_recv.at[d - 1], to, b)

    def root_z_wait(d):
        src = lax.rem(cz + 8 - d, 8)
        ref = rbuf.at[cx, src]
        return remote(ref, ref, z_send.at[d - 1], z_recv.at[d - 1], leaf_id(src, cx, core), b)

    def root_x(d):
        to = leaf_id(cz, lax.rem(cx + d, 4), core)
        ref = rbuf.at[cx]
        return remote(ref, ref, x_send.at[d - 1], x_recv.at[d - 1], to, b)

    def root_x_wait(d):
        src = lax.rem(cx + 4 - d, 4)
        ref = rbuf.at[src]
        return remote(ref, ref, x_send.at[d - 1], x_recv.at[d - 1], leaf_id(cz, src, core), b)

    def root_c(d):
        ref = rbuf.at[lax.rem(cx + 4 - d, 4)]
        return remote(ref, ref, c_send.at[d], c_recv.at[d], leaf_id(cz, cx, 1 - core), b)

    @pl.when(sender)
    def _():
        for d in range(1, 8):
            root_z(d).start()

    for h in range(2):
        v = pts[:, h * 128:(h + 1) * 128]
        rts[h * 128:(h + 1) * 128, :] = to_rows(v[:DIM], v[RAW:])

    near_chunk(CHUNKS - 1)

    wlane = lax.broadcasted_iota(jnp.int32, (RHS, 128), 1)
    for k, step in enumerate(STEPS):
        exists = (o + step >= 0) & (o + step < OWNERS)

        @pl.when(exists)
        def _():
            for c in range(CHUNKS):
                far_wait(c, k).wait_recv()

            @pl.loop(0, 8, unroll=8)
            def _(q):
                v = fin[k, q]
                even = k * 16 + 2 * q
                rows = to_rows(v[:DIM], v[RAW:])
                fs[even] = rows[:64]
                fs[even + 1] = rows[64:]
                w = v[DIM:RAW].astype(F32)
                left = jnp.where(wlane < 64, w, 0.0)
                right = jnp.where(wlane < 64, 0.0, w)
                wl[even] = left
                wr[even] = pltpu.roll(left, 64, axis=1)
                wl[even + 1] = pltpu.roll(right, 64, axis=1)
                wr[even + 1] = right

        @pl.when(jnp.logical_not(exists))
        def _():
            @pl.loop(k * 16, k * 16 + 16)
            def _(e):
                fs[e] = jnp.zeros((64, 128), BF16)
                wl[e] = jnp.zeros((RHS, 128), F32)
                wr[e] = jnp.zeros((RHS, 128), F32)

    lists = fl_v[...]

    def named(u):
        f = fl_s[0, u]
        owner = f // LEAVES
        step = owner - o
        at = (step + 2 - jnp.where(step > 0, 1, 0)) * LEAVES + f - owner * LEAVES
        hit = jnp.max(jnp.where(lists == f, 1.0, 0.0), axis=1, keepdims=True)
        return jnp.clip(at, 0, 63), hit * jnp.where(step == 0, 0.0, 1.0)

    for v in range(PAIRS):
        at0, hit0 = named(2 * v)
        at1, hit1 = named(2 * v + 1)
        sall[v * 128:v * 128 + 64, :] = fs[at0]
        sall[v * 128 + 64:v * 128 + 128, :] = fs[at1]
        wall[:, v * 128:(v + 1) * 128] = wl[at0] + wr[at1]
        mask[:, v * 128:(v + 1) * 128] = jnp.where(wlane < 64, hit0, hit1)

    def far_range(lo, hi):
        @pl.loop(lo, hi, step=2)
        def _(l):
            t = jnp.concatenate([skel_o[l], skel_o[l + 1]], axis=1)
            w0 = (wall[...] * mask[pl.ds(l, 1), :]).astype(BF16)
            w1 = (wall[...] * mask[pl.ds(l + 1, 1), :]).astype(BF16)
            x = jnp.dot(sall[:, :ROWS], t, preferred_element_type=F32)
            p = jnp.exp(x).astype(BF16)
            farsum[l] = jnp.dot(w0, p[:, :SKEL], preferred_element_type=F32)
            farsum[l + 1] = jnp.dot(w1, p[:, SKEL:], preferred_element_type=F32)

    @pl.when(sender)
    def _():
        for d in range(1, 8):
            root_z_wait(d).wait_recv()
        for d in range(1, 4):
            root_x(d).start()
        root_c(0).start()

    def scatter_copy(c, d):
        to = lax.rem(b + d, BLKS)
        return remote(part.at[to, pl.ds(c * QUAD, QUAD)], land.at[d - 1, pl.ds(c * QUAD, QUAD)],
                      s_send.at[c, d - 1], s_recv.at[c, d - 1], o, to)

    def far_down(c):
        for l in range(c * QUAD, (c + 1) * QUAD):
            total = near_o[l] + jnp.dot(farsum[l].astype(BF16), li[l], preferred_element_type=F32)
            total = total.astype(BF16)
            for d in range(BLKS):
                part[d, l] = total[:, d * 128:(d + 1) * 128]
        for d in (2, 1, 3):
            scatter_copy(c, d).start()

    far_range(0, FAR_A)
    @pl.when(sender)
    def _():
        for d in range(1, 4):
            root_x_wait(d).wait_recv()
            root_c(d).start()

    far_range(FAR_A, FAR_B)
    for c in range(FAR_B // QUAD):
        far_down(c)

    @pl.when(jnp.logical_not(sender))
    def _():
        for d in range(4):
            root_c(d).wait_recv()

    targets = rts[:, :ROWS]

    def root_group(i, acc):
        cols = []
        wgts = []
        for e in range(4):
            x = i // 2
            z = (i - 2 * x) * 4 + e
            p = leaf_id(z, x, parity)
            v = rbuf[x, z]
            cols.append(v)
            wgts.append(jnp.where(jnp.abs(p - o) > 2, v[DIM:RAW].astype(F32), 0.0).astype(BF16))
        xt = jnp.dot(targets, jnp.concatenate(cols, axis=1), preferred_element_type=F32)
        pt = jnp.exp(xt).astype(BF16)
        w = jnp.concatenate(wgts, axis=1)
        return acc + lax.dot_general(w, pt, NT, preferred_element_type=F32)

    rf = lax.fori_loop(0, 8, root_group, jnp.zeros((RHS, SKEL), F32), unroll=8).astype(BF16)

    rfs[b] = rf

    def root_sum(d):
        return remote(rfs.at[b], rfs.at[b], r_send.at[d - 1], r_recv.at[d - 1], o, lax.rem(b + d, BLKS))

    for d in range(1, BLKS):
        root_sum(d).start()
    far_range(FAR_B, LEAVES)
    for c in range(FAR_B // QUAD, QUADS):
        far_down(c)

    for d in range(1, BLKS):
        root_sum(d).wait_recv()
    field = rfs[0].astype(F32)
    for d in range(1, BLKS):
        field = field + rfs[d].astype(F32)
    field = field.astype(BF16)
    mine = pl.ds(pl.multiple_of(b * 128, 128), 128)
    for c in range(QUADS):
        group = range(c * QUAD, (c + 1) * QUAD)
        lifted = [jnp.dot(field, rt[l], preferred_element_type=F32).astype(BF16) for l in group]
        for d in range(1, BLKS):
            scatter_copy(c, d).wait_recv()
        for l, v in zip(group, lifted):
            total = jnp.dot(v, li[l, :, mine], preferred_element_type=F32)
            total = total + part[b, l].astype(F32)
            for d in range(BLKS - 1):
                total = total + land[d, l].astype(F32)
            out[l] = total

    @pl.when(has_high)
    def _():
        h_up.wait_send()

    @pl.when(has_low)
    def _():
        h_down.wait_send()

    for c in range(CHUNKS):
        for k, step in enumerate(STEPS):
            @pl.when((o + step >= 0) & (o + step < OWNERS))
            def _():
                far_copy(c, k).wait_send()
        for d in (1, 2, 3):
            gather_copy(c, d).wait_send()

    for d in range(1, BLKS):
        root_sum(d).wait_send()
        for c in range(QUADS):
            scatter_copy(c, d).wait_send()

    @pl.when(sender)
    def _():
        for d in range(1, 8):
            root_z(d).wait_send()
        for d in range(1, 4):
            root_x(d).wait_send()
        for d in range(4):
            root_c(d).wait_send()


def on_device(points, charges, leaf_interp, root_interp, skeleton_index, root_index, near_list, far_list, far_count):
    vmem = pl.BlockSpec(memory_space=pltpu.VMEM)
    smem = pl.BlockSpec(memory_space=pltpu.SMEM)
    hbm = pl.BlockSpec(memory_space=pl.ANY)
    dma = pltpu.SemaphoreType.DMA

    out = pl.pallas_call(
        potential_kernel,
        out_shape=jax.ShapeDtypeStruct((LEAVES, RHS, PTS), F32),
        in_specs=[hbm, hbm, smem, smem, vmem, vmem, vmem, hbm, hbm],
        out_specs=vmem,
        scratch_shapes=[
            pltpu.VMEM((DIM, LEAVES, PTS), BF16),
            pltpu.VMEM((RHS, LEAVES, PTS), BF16),
            pltpu.VMEM((LEAVES, RAW, PTS), BF16),
            pltpu.VMEM((BLKS, LEAVES, ROWS, PTS), BF16),
            pltpu.VMEM((2, HALO, RAW, PTS), BF16),
            pltpu.VMEM((2 * HALO + LEAVES, 128, 128), BF16),
            pltpu.VMEM((2 * HALO + LEAVES, RHS, 128), BF16),
            pltpu.VMEM((LEAVES, SKEL, BLKS * PTS), BF16),
            pltpu.VMEM((LEAVES, SKEL, SKEL), BF16),
            pltpu.VMEM((8, ROWS, 128), BF16),
            pltpu.VMEM((4, 8, ROWS, 128), BF16),
            pltpu.VMEM((4, 8, ROWS, 128), BF16),
            pltpu.VMEM((LEAVES, RHS, BLKS * PTS), F32),
            pltpu.VMEM((LEAVES, ROWS, SKEL), BF16),
            pltpu.VMEM((64, 64, 128), BF16),
            pltpu.VMEM((64, RHS, 128), F32),
            pltpu.VMEM((64, RHS, 128), F32),
            pltpu.VMEM((SKEL, 128), BF16),
            pltpu.VMEM((PAIRS * 128, 128), BF16),
            pltpu.VMEM((RHS, PAIRS * 128), F32),
            pltpu.VMEM((LEAVES, PAIRS * 128), F32),
            pltpu.VMEM((LEAVES, RHS, SKEL), F32),
            pltpu.VMEM((BLKS, LEAVES, RHS, PTS), BF16),
            pltpu.VMEM((BLKS - 1, LEAVES, RHS, PTS), BF16),
            pltpu.VMEM((BLKS, RHS, SKEL), BF16),
            dma, dma, dma, dma,
            dma((CHUNKS, 3)), dma((CHUNKS, 3)),
            dma((2,)), dma((2,)),
            dma((CHUNKS, 4)), dma((CHUNKS, 4)),
            dma((7,)), dma((7,)), dma((3,)), dma((3,)), dma((4,)), dma((4,)),
            dma((QUADS, 3)), dma((QUADS, 3)), dma((3,)), dma((3,)),
        ],
        compiler_params=pltpu.CompilerParams(
            collective_id=0, has_side_effects=True, vmem_limit_bytes=VMEM_LIMIT),
    )(points, charges, near_list, far_list, far_list, skeleton_index, root_index, leaf_interp, root_interp)
    return jnp.transpose(out, (1, 0, 2))


def solution(mesh):
    placed = (
        P(None, "leaf", "blk"),
        P(None, "leaf", "blk"),
        P("leaf", None, None),
        P("leaf", None, None),
        P("leaf", None),
        P("leaf", None),
        P("leaf", None),
        P("leaf", None),
        P("leaf"),
    )
    return jax.shard_map(
        on_device, mesh=mesh, in_specs=placed, out_specs=P(None, "leaf", "blk"), check_vma=False
    )
```
